32 devices in a mesh: seq: 8 (over y, x, core), dp: 4 (over z).
Axes of the slice: x: 2, y: 2, z: 4, core: 2. Of those that a mesh axis runs over, the one named last changes fastest.
Arguments:
- queries: bfloat16 [4, 1024, 2048], P('dp', 'seq'), may hold values from -6 to 6
- keys: bfloat16 [4, 1024, 2048], P('dp', 'seq'), may hold values from -6 to 6
- values: bfloat16 [4, 1024, 2048], P('dp', 'seq'), may hold values from -6 to 6
- master: float32 [2048, 1024], P(('seq', 'dp')), may hold values from -0.24 to 0.24
- moment: float32 [2048, 1024], P(('seq', 'dp')), may hold values from -0.06 to 0.06
- second: float32 [2048, 1024], P(('seq', 'dp')), may hold values from 1e-06 to 0.0001
- gradient: float32 [2048, 1024], P(('seq', 'dp')), may hold values from -0.18 to 0.18
Outputs:
- projected: bfloat16 [4, 1024, 1024], P('dp', 'seq')
- new_master: float32 [2048, 1024], P(('seq', 'dp'))
The draws below stay inside these ranges and needn't reach their ends.
All inputs are finite; a program needn't handle non-finite values.
Results may differ from the reference program's by a relative error of at most 0.0063.
Values may be sent and summed in bfloat16 or wider, within the bound.
No kernel may reach another device: no remote copies, remote signals or barrier semaphores. Data moves between devices by JAX's collectives and lax.ppermute only.
A program may use at most 64 MiB of HBM per device.

```python
import math
import jax
import jax.numpy as jnp
from jax import lax

HEADS = 16
HEAD_DIM = 128
D_OUT = 1024
LENGTH = 1024
SEQS = 4


def drawn(key, which):
    base = jax.random.normal(jax.random.fold_in(key, which), (SEQS, LENGTH, HEADS, HEAD_DIM), jnp.float32)
    base = jnp.clip(base, -6.0, 6.0)
    return base.reshape(SEQS, LENGTH, HEADS * HEAD_DIM).astype(jnp.bfloat16)


def draw_queries(key, part):
    return drawn(key, 1)


def draw_keys(key, part):
    return drawn(key, 2)


def block_levels(rng, extent, split, least, high):
    factor_of = 1.0
    for dim, blocks in split:
        heights = jax.random.uniform(jax.random.fold_in(jax.random.fold_in(rng, 6), dim), (blocks,), jnp.float32, least / len(split), high / len(split))
        factor_of = factor_of * jnp.repeat(jnp.exp(heights), extent[dim] // blocks).reshape((-1,) + (1,) * (len(extent) - 1 - dim))
    return factor_of


def scatter_about(rng, shape, width, limit, cuts=(), kind=jnp.bfloat16):
    factor_of = block_levels(rng, shape, cuts, -0.22, 0.18) if cuts else 1.0
    result = jax.random.normal(rng, shape, jnp.float32) * width * factor_of
    return jnp.minimum(jnp.maximum(result, -limit), limit).astype(kind)


def setup_inputs(seed: int = 0) -> dict:
    key_list = jax.random.split(jax.random.key(seed), 8)
    queries = draw_queries(jax.random.fold_in(key_list[7], 71), 0)
    keys = draw_keys(jax.random.fold_in(key_list[7], 71), 0)
    values = scatter_about(key_list[2], (SEQS, LENGTH, HEADS * HEAD_DIM), 1.0, 6.0, ((0, 4), (1, 8)))
    master = scatter_about(key_list[3], (HEADS * HEAD_DIM, D_OUT), 0.04, 0.24, ((0, 32),), jnp.float32)
    moment = scatter_about(key_list[4], (HEADS * HEAD_DIM, D_OUT), 0.01, 0.06, ((0, 32),), jnp.float32)
    second = jnp.clip(jnp.exp(math.log(0.0001) - 4.6051702 * jax.random.uniform(key_list[5], (HEADS * HEAD_DIM, D_OUT), jnp.float32) ** block_levels(key_list[5], (HEADS * HEAD_DIM, D_OUT), ((0, 32),), -0.2, 0.2)), 9.999999974752427e-07, 0.0001)
    gradient = scatter_about(key_list[6], (HEADS * HEAD_DIM, D_OUT), 0.03, 0.18, ((0, 32),), jnp.float32)
    return dict(queries=queries, keys=keys, values=values, master=master, moment=moment, second=second, gradient=gradient)


beta_first = 0.9
beta_second = 0.999
learning_rate = 0.1
weight_decay = 0.1
epsilon = 1e-08
step_count = 10.0

def adamw(master, moment, second, gradient):
    moment_new = beta_first * moment + (1.0 - beta_first) * gradient
    second_new = beta_second * second + (1.0 - beta_second) * gradient * gradient
    moment_hat = moment_new / (1.0 - beta_first ** step_count)
    second_hat = second_new / (1.0 - beta_second ** step_count)
    return master - learning_rate * (moment_hat / (jnp.sqrt(second_hat) + epsilon) + weight_decay * master)

def attend_head(triple):
    query_rows, key_rows, value_rows = triple
    scores = jnp.dot(query_rows, key_rows.T, preferred_element_type=jnp.float32) * HEAD_DIM ** (-0.5)
    positions = jnp.arange(LENGTH)
    causal = positions[:, None] >= positions[None, :]
    scores = jnp.where(causal, scores, -jnp.inf)
    highest = lax.optimization_barrier(jnp.max(scores, axis=1, keepdims=True))
    expons = jnp.exp(scores - highest)
    denominator = lax.optimization_barrier(jnp.sum(expons, axis=1, keepdims=True))
    probs = (expons / denominator).astype(jnp.bfloat16)
    return jnp.dot(probs, value_rows, preferred_element_type=jnp.float32).astype(jnp.bfloat16)

def heads_first(array):
    return array.reshape(SEQS, LENGTH, HEADS, HEAD_DIM).transpose(0, 2, 1, 3).reshape(SEQS * HEADS, LENGTH, HEAD_DIM)

def reference(queries, keys, values, master, moment, second, gradient):
    attended = lax.map(attend_head, (heads_first(queries), heads_first(keys), heads_first(values)))
    attended = attended.reshape(SEQS, HEADS, LENGTH, HEAD_DIM).transpose(0, 2, 1, 3).reshape(SEQS * LENGTH, HEADS * HEAD_DIM)
    new_master = adamw(master, moment, second, gradient)
    weight = new_master.astype(jnp.bfloat16)
    projected = jnp.dot(attended, weight, preferred_element_type=jnp.float32).astype(jnp.bfloat16)
    return (projected.reshape(SEQS, LENGTH, D_OUT), new_master)
```

```python
import jax
import jax.numpy as jnp
from jax import lax
from jax.sharding import PartitionSpec as P

HEAD_DIM = 128


beta_first = 0.9
beta_second = 0.999
learning_rate = 0.1
weight_decay = 0.1
epsilon = 1e-08
step_count = 10.0


def adamw(master, moment, second, gradient):
    moment_new = beta_first * moment + (1.0 - beta_first) * gradient
    second_new = beta_second * second + (1.0 - beta_second) * gradient * gradient
    moment_hat = moment_new / (1.0 - beta_first**step_count)
    second_hat = second_new / (1.0 - beta_second**step_count)
    return master - learning_rate * (
        moment_hat / (jnp.sqrt(second_hat) + epsilon) + weight_decay * master
    )


def causal_attention(head_queries, head_keys, head_values):
    seq_length = head_queries.shape[0]
    block_rows = min(512, seq_length)
    results = []
    for first_row in range(0, seq_length, block_rows):
        last_key = first_row + block_rows
        query_block = head_queries[first_row:last_key]
        scores = jnp.einsum(
            "qhd,khd->hqk", query_block, head_keys[:last_key], preferred_element_type=jnp.float32
        )
        scores = scores * HEAD_DIM ** (-0.5)
        causal = (first_row + jnp.arange(block_rows))[:, None] >= jnp.arange(last_key)[None, :]
        scores = jnp.where(causal[None], scores, -jnp.inf)
        highest = jnp.max(scores, axis=2, keepdims=True)
        expons = jnp.exp(scores - highest)
        denominator = jnp.sum(expons, axis=2, keepdims=True)
        probs = (expons / denominator).astype(jnp.bfloat16)
        attended = jnp.einsum(
            "hqk,khd->qhd", probs, head_values[:last_key], preferred_element_type=jnp.float32
        )
        results.append(attended.astype(jnp.bfloat16))
    return jnp.concatenate(results, axis=0)


def swap(array, axis, count, distance):
    return lax.ppermute(array, axis, [(i, i ^ distance) for i in range(count)])


def make_body(seq_count, dp_count):
    def body(queries, keys, values, master, moment, second, gradient):
        tok_rows = queries.shape[1]
        feature_count = queries.shape[2]
        own_features = feature_count // seq_count
        out_features = master.shape[1]
        me = lax.axis_index("seq")
        place = lax.axis_index("dp")

        packed = jnp.stack([queries[0], keys[0], values[0]]).reshape(
            3, tok_rows, seq_count, own_features
        )
        packed = packed.transpose(2, 0, 1, 3)
        parts = []
        for distance in range(seq_count):
            part = lax.dynamic_index_in_dim(packed, me ^ distance, 0, keepdims=False)
            parts.append(swap(part, "seq", seq_count, distance) if distance else part)

        new_master = adamw(master, moment, second, gradient)
        rows = new_master.astype(jnp.bfloat16)[None]
        distance = 1
        while distance < dp_count:
            rows = jnp.concatenate([rows, swap(rows, "dp", dp_count, distance)], axis=0)
            distance *= 2
        rows = jnp.take(rows, place ^ jnp.arange(dp_count), axis=0)
        own_weight = rows.reshape(own_features, out_features)
        their_weight = swap(own_weight, "seq", seq_count, 1)

        whole = jnp.zeros((seq_count, 3, tok_rows, own_features), queries.dtype)
        for distance in range(seq_count):
            whole = lax.dynamic_update_index_in_dim(whole, parts[distance], me ^ distance, 0)
        whole = whole.transpose(1, 0, 2, 3).reshape(
            3, seq_count * tok_rows, own_features // HEAD_DIM, HEAD_DIM
        )
        attended = causal_attention(whole[0], whole[1], whole[2])

        pairs = attended.reshape(seq_count // 2, 2, tok_rows, own_features)
        core = me % 2
        kept = lax.dynamic_index_in_dim(pairs, core, 1, keepdims=False)
        given = lax.dynamic_index_in_dim(pairs, 1 - core, 1, keepdims=False)
        taken = swap(given, "seq", seq_count, 1)
        partial = jnp.einsum(
            "crf,fo->cro", kept, own_weight, preferred_element_type=jnp.float32
        ) + jnp.einsum("crf,fo->cro", taken, their_weight, preferred_element_type=jnp.float32)
        projected = lax.dynamic_index_in_dim(partial, me // 2, 0, keepdims=False)
        for distance in range(1, seq_count // 2):
            sent = lax.dynamic_index_in_dim(partial, (me // 2) ^ distance, 0, keepdims=False)
            got = swap(sent.astype(jnp.bfloat16), "seq", seq_count, 2 * distance)
            projected = projected + got.astype(jnp.float32)
        return (projected.astype(jnp.bfloat16)[None], new_master)

    return body


def solution(mesh):
    tokens = P("dp", "seq", None)
    rows = P(("seq", "dp"), None)
    return jax.shard_map(
        make_body(mesh.shape["seq"], mesh.shape["dp"]),
        mesh=mesh,
        in_specs=(tokens,) * 3 + (rows,) * 4,
        out_specs=(tokens, rows),
        check_vma=False,
    )
```

```python
import functools
import math

import jax
import jax.numpy as jnp
from jax import lax
from jax.experimental import pallas as pl
from jax.experimental.pallas import tpu as pltpu
from jax.sharding import PartitionSpec as P

HEAD_DIM = 128
LANES = 128


beta_first = 0.9
beta_second = 0.999
learning_rate = 0.1
weight_decay = 0.1
epsilon = 1e-08
step_count = 10.0


def adamw(master, moment, second, gradient):
    moment_new = beta_first * moment + (1.0 - beta_first) * gradient
    second_new = beta_second * second + (1.0 - beta_second) * gradient * gradient
    moment_hat = moment_new / (1.0 - beta_first**step_count)
    second_hat = second_new / (1.0 - beta_second**step_count)
    return master - learning_rate * (
        moment_hat / (jnp.sqrt(second_hat) + epsilon) + weight_decay * master
    )


def swap(array, axis, count, distance):
    return lax.ppermute(array, axis, [(i, i ^ distance) for i in range(count)])


SMEM = pl.BlockSpec(memory_space=pltpu.SMEM)
VMEM = pl.BlockSpec(memory_space=pltpu.VMEM)
PARAMS = pltpu.CompilerParams(vmem_limit_bytes=32 * 1024 * 1024)


def pack_kernel(me_ref, *refs):
    arrays, parts = refs[:3], refs[3:]
    width = parts[0].shape[2]
    for distance, part in enumerate(parts):
        first = pl.multiple_of((me_ref[0] ^ distance) * width, width)
        for which, array in enumerate(arrays):
            part[which] = array[0, :, pl.ds(first, width)]


def pack(me, arrays, count):
    _, rows, features = arrays[0].shape
    part = jax.ShapeDtypeStruct((3, rows, features // count), arrays[0].dtype)
    size = 2 * 3 * rows * features * 2
    return pl.pallas_call(
        pack_kernel,
        out_shape=[part] * count,
        in_specs=[SMEM] + [VMEM] * 3,
        out_specs=[VMEM] * count,
        compiler_params=PARAMS,
        cost_estimate=pl.CostEstimate(flops=0, bytes_accessed=size, transcendentals=0),
        name="pack",
    )(me, *arrays)


def attend_kernel(count, block, me_ref, *refs):
    parts = refs[:count]
    kept, given, queries, keys, values, attended = refs[count:]
    rows = parts[0].shape[1]
    heads = values.shape[0]
    length = queries.shape[0]
    me = me_ref[0]
    for head in range(heads):
        values[head, :, HEAD_DIM:] = jnp.ones((length, LANES), values.dtype)
    for distance, part in enumerate(parts):
        at = pl.ds(pl.multiple_of((me ^ distance) * rows, rows), rows)
        queries[at, :] = part[0]
        keys[at, :] = part[1]
        for head in range(heads):
            values[head, at, :HEAD_DIM] = part[2, :, head * HEAD_DIM : (head + 1) * HEAD_DIM]
    scale = HEAD_DIM ** (-0.5) * math.log2(math.e)
    for first in range(0, length, block):
        last = first + block
        causal = lax.broadcasted_iota(jnp.int32, (block, block), 0) >= lax.broadcasted_iota(
            jnp.int32, (block, block), 1
        )
        for head in range(heads):
            columns = slice(head * HEAD_DIM, (head + 1) * HEAD_DIM)
            scores = lax.dot_general(
                queries[first:last, columns],
                keys[:last, columns],
                (((1,), (1,)), ((), ())),
                preferred_element_type=jnp.float32,
            )
            near = jnp.where(causal, scores[:, first:], -jnp.inf)
            highest = jnp.max(near, axis=1, keepdims=True)
            if first:
                far = scores[:, :first]
                highest = jnp.maximum(highest, jnp.max(far, axis=1, keepdims=True))
            expons = jnp.exp2((near - highest) * scale).astype(jnp.bfloat16)
            total = jnp.dot(expons, values[head, first:last], preferred_element_type=jnp.float32)
            if first:
                expons = jnp.exp2((far - highest) * scale).astype(jnp.bfloat16)
                total = total + jnp.dot(
                    expons, values[head, :first], preferred_element_type=jnp.float32
                )
            attended[first:last, columns] = (total[:, :HEAD_DIM] / total[:, HEAD_DIM:]).astype(
                attended.dtype
            )
    for distance in range(count // 2):
        pair = ((me // 2) ^ distance) * 2
        here, there = pair + me % 2, pair + 1 - me % 2
        at = slice(distance * rows, (distance + 1) * rows)
        kept[at, :] = attended[pl.ds(pl.multiple_of(here * rows, rows), rows), :]
        given[at, :] = attended[pl.ds(pl.multiple_of(there * rows, rows), rows), :]


def attend(me, parts):
    count = len(parts)
    _, rows, features = parts[0].shape
    length = count * rows
    heads = features // HEAD_DIM
    kind = parts[0].dtype
    half = jax.ShapeDtypeStruct((length // 2, features), kind)
    return pl.pallas_call(
        functools.partial(attend_kernel, count, min(256, length)),
        out_shape=[half, half],
        in_specs=[SMEM] + [VMEM] * count,
        out_specs=[VMEM] * 2,
        scratch_shapes=[
            pltpu.VMEM((length, features), kind),
            pltpu.VMEM((length, features), kind),
            pltpu.VMEM((heads, length, HEAD_DIM + LANES), kind),
            pltpu.VMEM((length, features), kind),
        ],
        compiler_params=PARAMS,
        cost_estimate=pl.CostEstimate(
            flops=4 * length * length * features,
            bytes_accessed=8 * length * features,
            transcendentals=length * length * heads // 2,
        ),
        name="attend",
    )(me, *parts)


def project_kernel(kept, taken, own_weight, their_weight, here, *sent):
    rows = here.shape[0]
    product = jnp.dot(kept[...], own_weight[...], preferred_element_type=jnp.float32)
    product += jnp.dot(taken[...], their_weight[...], preferred_element_type=jnp.float32)
    here[...] = product[:rows]
    for distance, block in enumerate(sent, 1):
        block[...] = product[distance * rows : (distance + 1) * rows].astype(block.dtype)


def project(kept, taken, own_weight, their_weight, rows):
    total, features = kept.shape
    outs = own_weight.shape[1]
    return pl.pallas_call(
        project_kernel,
        out_shape=[jax.ShapeDtypeStruct((rows, outs), jnp.float32)]
        + [jax.ShapeDtypeStruct((rows, outs), kept.dtype)] * (total // rows - 1),
        in_specs=[VMEM] * 4,
        out_specs=[VMEM] * (total // rows),
        compiler_params=PARAMS,
        cost_estimate=pl.CostEstimate(
            flops=4 * total * features * outs,
            bytes_accessed=4 * total * features + 4 * features * outs + 2 * total * outs,
            transcendentals=0,
        ),
        name="project",
    )(kept, taken, own_weight, their_weight)


def make_body(seq_count, dp_count):
    def body(queries, keys, values, master, moment, second, gradient):
        tok_rows = queries.shape[1]
        own_features = queries.shape[2] // seq_count
        out_features = master.shape[1]
        me = lax.axis_index("seq")
        place = lax.axis_index("dp")
        me_array = me.astype(jnp.int32).reshape(1)

        parts = pack(me_array, (queries, keys, values), seq_count)
        parts = [
            swap(part, "seq", seq_count, distance) if distance else part
            for distance, part in enumerate(parts)
        ]

        new_master = adamw(master, moment, second, gradient)
        rows = new_master.astype(jnp.bfloat16)[None]
        distance = 1
        while distance < dp_count:
            rows = jnp.concatenate([rows, swap(rows, "dp", dp_count, distance)], axis=0)
            distance *= 2
        rows = jnp.take(rows, place ^ jnp.arange(dp_count), axis=0)
        own_weight = rows.reshape(own_features, out_features)
        their_weight = swap(own_weight, "seq", seq_count, 1)

        kept, given = attend(me_array, parts)
        taken = swap(given, "seq", seq_count, 1)
        here, *sent = project(kept, taken, own_weight, their_weight, tok_rows)
        projected = here
        for distance, block in enumerate(sent, 1):
            projected += swap(block, "seq", seq_count, 2 * distance).astype(jnp.float32)
        return (projected.astype(jnp.bfloat16)[None], new_master)

    return body


def solution(mesh):
    tokens = P("dp", "seq", None)
    rows = P(("seq", "dp"), None)
    return jax.shard_map(
        make_body(mesh.shape["seq"], mesh.shape["dp"]),
        mesh=mesh,
        in_specs=(tokens,) * 3 + (rows,) * 4,
        out_specs=(tokens, rows),
        check_vma=False,
    )
```

```python
import functools
import math

import jax
import jax.numpy as jnp
from jax import lax
from jax.experimental import pallas as pl
from jax.experimental.pallas import tpu as pltpu
from jax.sharding import PartitionSpec as P

HEAD_DIM = 128
LANES = 128


beta_first = 0.9
beta_second = 0.999
learning_rate = 0.1
weight_decay = 0.1
epsilon = 1e-08
step_count = 10.0


def adamw(master, moment, second, gradient):
    moment_new = beta_first * moment + (1.0 - beta_first) * gradient
    second_new = beta_second * second + (1.0 - beta_second) * gradient * gradient
    moment_hat = moment_new / (1.0 - beta_first**step_count)
    second_hat = second_new / (1.0 - beta_second**step_count)
    return master - learning_rate * (
        moment_hat / (jnp.sqrt(second_hat) + epsilon) + weight_decay * master
    )


def swap(array, axis, count, distance):
    return lax.ppermute(array, axis, [(i, i ^ distance) for i in range(count)])


SMEM = pl.BlockSpec(memory_space=pltpu.SMEM)
VMEM = pl.BlockSpec(memory_space=pltpu.VMEM)
HBM = pl.BlockSpec(memory_space=pltpu.HBM)
PARAMS = pltpu.CompilerParams(vmem_limit_bytes=32 * 1024 * 1024)


def in_hbm(array):
    return pltpu.with_memory_space_constraint(array, pltpu.HBM)


def like(shape, array):
    return jax.ShapeDtypeStruct(shape, array.dtype)


def cost(moved, flops=0, transcendentals=0):
    return pl.CostEstimate(
        flops=flops, bytes_accessed=moved, transcendentals=transcendentals
    )


def pack_kernel(me_ref, queries, keys, values, *refs):
    parts, sems = refs[:-1], refs[-1]
    chips = len(parts) // 2
    width = parts[0].shape[1]
    copies = []
    for which, array in enumerate((keys, values, queries)):
        for distance in range(chips):
            chip = (me_ref[0] // 2) ^ distance
            at = pl.ds(pl.multiple_of(chip * width, width), width)
            part = parts[distance] if which == 2 else parts[chips + distance].at[which]
            sem = sems.at[which * chips + distance]
            copies.append(pltpu.make_async_copy(array.at[0, :, at], part, sem))
    for copy in copies:
        copy.start()
    for copy in copies:
        copy.wait()


def pack(me, queries, keys, values, chips):
    _, rows, features = queries.shape
    width = features // chips
    parts = pl.pallas_call(
        pack_kernel,
        out_shape=[like((rows, width), queries)] * chips
        + [like((2, rows, width), queries)] * chips,
        in_specs=[SMEM] + [HBM] * 3,
        out_specs=[VMEM] * (2 * chips),
        scratch_shapes=[pltpu.SemaphoreType.DMA((3 * chips,))],
        compiler_params=PARAMS,
        cost_estimate=cost(12 * rows * features),
        name="pack",
    )(me, *map(in_hbm, (queries, keys, values)))
    return parts[:chips], parts[chips:]


def update_kernel(*refs):
    arrays, (new_master, weight), held, sems = refs[:4], refs[4:6], refs[6], refs[7]
    copies = [
        pltpu.make_async_copy(array, held.at[index], sems.at[index])
        for index, array in enumerate(arrays)
    ]
    for copy in copies:
        copy.start()
    for copy in copies:
        copy.wait()
    result = adamw(held[0], held[1], held[2], held[3])
    new_master[...] = result
    weight[...] = result.astype(weight.dtype)


def update(*arrays):
    shape, kind = arrays[0].shape, arrays[0].dtype
    return pl.pallas_call(
        update_kernel,
        out_shape=[like(shape, arrays[0]), jax.ShapeDtypeStruct(shape, jnp.bfloat16)],
        in_specs=[HBM] * 4,
        out_specs=[VMEM] * 2,
        scratch_shapes=[pltpu.VMEM((4, *shape), kind), pltpu.SemaphoreType.DMA((4,))],
        compiler_params=PARAMS,
        cost_estimate=cost(22 * arrays[0].size),
        name="update",
    )(*map(in_hbm, arrays))


def merge_kernel(index_ref, *refs):
    pieces, whole = refs[:-1], refs[-1]
    for distance, piece in enumerate(pieces):
        whole[:, index_ref[0] ^ distance] = piece[...]


def merge(index, pieces):
    shape = (pieces[0].shape[0], len(pieces)) + pieces[0].shape[1:]
    return pl.pallas_call(
        merge_kernel,
        out_shape=like(shape, pieces[0]),
        in_specs=[SMEM] + [VMEM] * len(pieces),
        out_specs=VMEM,
        compiler_params=PARAMS,
        cost_estimate=cost(4 * len(pieces) * pieces[0].size),
        name="merge",
    )(index, *pieces)


def stack_kernel(*refs):
    pieces, stacked = refs[:-1], refs[-1]
    for index, piece in enumerate(pieces):
        stacked[index] = piece[...]


def stack(pieces):
    return pl.pallas_call(
        stack_kernel,
        out_shape=like((len(pieces), *pieces[0].shape), pieces[0]),
        in_specs=[VMEM] * len(pieces),
        out_specs=VMEM,
        compiler_params=PARAMS,
        cost_estimate=cost(4 * len(pieces) * pieces[0].size),
        name="stack",
    )(*pieces)


def gather_kernel(me_ref, own, other, keys, values):
    chips, _, rows, _ = own.shape
    heads, length, _ = values.shape
    for head in range(heads):
        values[head, :, HEAD_DIM:] = jnp.ones((length, LANES), values.dtype)
    for distance in range(chips):
        for core, pair in enumerate((own, other)):
            block = me_ref[0] ^ (2 * distance + core)
            at = pl.ds(pl.multiple_of(block * rows, rows), rows)
            keys[at, :] = pair[distance, 0]
            for head in range(heads):
                values[head, at, :HEAD_DIM] = pair[
                    distance, 1, :, head * HEAD_DIM : (head + 1) * HEAD_DIM
                ]


def gather(me, own, other):
    chips, _, rows, width = own.shape
    length = 2 * chips * rows
    return pl.pallas_call(
        gather_kernel,
        out_shape=[
            like((length, width), own),
            like((width // HEAD_DIM, length, HEAD_DIM + LANES), own),
        ],
        in_specs=[SMEM] + [VMEM] * 2,
        out_specs=[VMEM] * 2,
        compiler_params=PARAMS,
        cost_estimate=cost(10 * length * width),
        name="gather",
    )(me, own, other)


def attend_kernel(chips, me_ref, *refs):
    parts, (keys, values, attended, queries, result) = refs[:chips], refs[chips:]
    rows, width = parts[0].shape
    near = 2 * rows
    chip, core = me_ref[0] // 2, me_ref[0] % 2
    for distance, part in enumerate(parts):
        at = pl.ds(pl.multiple_of((chip ^ distance) * rows, rows), rows)
        queries[at, :] = part[...]
    causal = core * rows + lax.broadcasted_iota(
        jnp.int32, (rows, near), 0
    ) >= lax.broadcasted_iota(jnp.int32, (rows, near), 1)
    scale = HEAD_DIM ** (-0.5) * math.log2(math.e)
    for head in range(width // HEAD_DIM):
        columns = slice(head * HEAD_DIM, (head + 1) * HEAD_DIM)
        scores = []
        for c in range(chips):
            score = lax.dot_general(
                queries[c * rows :, columns],
                keys[c * near : (c + 1) * near, columns],
                (((1,), (1,)), ((), ())),
                preferred_element_type=jnp.float32,
            )
            masked = jnp.where(causal, score[:rows], -jnp.inf)
            scores.append(jnp.concatenate([masked, score[rows:]], axis=0) if c < chips - 1 else masked)
        highest = []
        for block in range(chips):
            best = scores[0][block * rows : (block + 1) * rows]
            for c in range(1, block + 1):
                best = jnp.maximum(best, scores[c][(block - c) * rows : (block - c + 1) * rows])
            highest.append(jnp.max(best, axis=1, keepdims=True))
        highest = jnp.concatenate(highest, axis=0)
        totals = None
        for c in range(chips):
            expons = jnp.exp2((scores[c] - highest[c * rows :]) * scale).astype(jnp.bfloat16)
            total = jnp.dot(
                expons, values[head, c * near : (c + 1) * near], preferred_element_type=jnp.float32
            )
            if c:
                total += totals[rows:]
            totals = total
            result[c * rows : (c + 1) * rows, columns] = (
                totals[:rows, :HEAD_DIM] / totals[:rows, HEAD_DIM:]
            ).astype(result.dtype)
    half = width // 2
    for distance in range(chips):
        at = pl.ds(pl.multiple_of((chip ^ distance) * rows, rows), rows)
        for part in range(2):
            attended[part, distance * rows : (distance + 1) * rows, :] = result[
                at, part * half : (part + 1) * half
            ]


def attend(me, parts, keys, values):
    chips = len(parts)
    rows, width = parts[0].shape
    length = keys.shape[0]
    total = chips * rows
    return pl.pallas_call(
        functools.partial(attend_kernel, chips),
        out_shape=like((2, total, width // 2), keys),
        in_specs=[SMEM] + [VMEM] * (chips + 2),
        out_specs=VMEM,
        scratch_shapes=[pltpu.VMEM((total, width), keys.dtype)] * 2,
        compiler_params=PARAMS,
        cost_estimate=cost(
            6 * length * width + 4 * total * width,
            4 * total * length * width,
            total * length * (width // HEAD_DIM),
        ),
        name="attend",
    )(me, *parts, keys, values)


def project_kernel(me_ref, attended, own_weight, their_weight, here, *sent):
    rows = here.shape[0]
    core = me_ref[0] % 2
    product = jnp.dot(attended[core], own_weight[...], preferred_element_type=jnp.float32)
    product += jnp.dot(attended[1 - core], their_weight[...], preferred_element_type=jnp.float32)
    here[...] = product[:rows]
    for distance, block in enumerate(sent, 1):
        block[...] = product[distance * rows : (distance + 1) * rows].astype(block.dtype)


def project(me, attended, own_weight, their_weight, rows):
    _, total, features = attended.shape
    outs = own_weight.shape[1]
    return pl.pallas_call(
        project_kernel,
        out_shape=[jax.ShapeDtypeStruct((rows, outs), jnp.float32)]
        + [like((rows, outs), attended)] * (total // rows - 1),
        in_specs=[SMEM] + [VMEM] * 3,
        out_specs=[VMEM] * (total // rows),
        compiler_params=PARAMS,
        cost_estimate=cost(
            4 * total * features + 4 * features * outs + 2 * total * outs,
            4 * total * features * outs,
        ),
        name="project",
    )(me, attended, own_weight, their_weight)


def make_body(seq_count, dp_count):
    chips = seq_count // 2

    def body(queries, keys, values, master, moment, second, gradient):
        own_features = queries.shape[2] // seq_count
        out_features = master.shape[1]
        me = lax.axis_index("seq").astype(jnp.int32).reshape(1)
        place = lax.axis_index("dp").astype(jnp.int32)

        query_parts, pair_parts = pack(me, queries, keys, values, chips)
        pairs = [pair_parts[0]]
        pairs += [swap(pair_parts[d], "seq", seq_count, 2 * d) for d in range(1, chips)]

        state, _ = lax.optimization_barrier(((master, moment, second, gradient), pair_parts))
        new_master, weight = update(*state)
        weight = weight[None]
        distance = dp_count // 2
        while distance > 1:
            theirs = swap(weight, "dp", dp_count, distance)
            pairs, theirs = lax.optimization_barrier((pairs, theirs))
            weight = merge((place // distance % 2).reshape(1), [weight, theirs])
            weight = weight.reshape(-1, *weight.shape[2:])
            distance //= 2
        theirs = swap(weight, "dp", dp_count, 1)
        own_pairs = stack(pairs)
        other_pairs = swap(own_pairs, "seq", seq_count, 1)
        sent, _ = lax.optimization_barrier((query_parts[1:], pairs))
        own_queries = [query_parts[0]]
        own_queries += [swap(part, "seq", seq_count, 2 * d) for d, part in enumerate(sent, 1)]
        own_queries, other_pairs, theirs = lax.optimization_barrier(
            (own_queries, other_pairs, theirs)
        )
        weight = merge((place % 2).reshape(1), [weight, theirs])
        own_weight = weight.reshape(own_features, out_features)
        their_weight = swap(own_weight, "seq", seq_count, 1)

        all_keys, all_values = gather(me, own_pairs, other_pairs)
        attended = attend(me, own_queries, all_keys, all_values)
        here, *sent = project(me, attended, own_weight, their_weight, queries.shape[1])
        projected = here
        for d, block in enumerate(sent, 1):
            projected += swap(block, "seq", seq_count, 2 * d).astype(jnp.float32)
        return (projected.astype(jnp.bfloat16)[None], new_master)

    return body


def solution(mesh):
    tokens = P("dp", "seq", None)
    rows = P(("seq", "dp"), None)
    return jax.shard_map(
        make_body(mesh.shape["seq"], mesh.shape["dp"]),
        mesh=mesh,
        in_specs=(tokens,) * 3 + (rows,) * 4,
        out_specs=(tokens, rows),
        check_vma=False,
    )
```

```python
import functools
import math

import jax
import jax.numpy as jnp
from jax import lax
from jax.experimental import pallas as pl
from jax.experimental.pallas import tpu as pltpu
from jax.sharding import PartitionSpec as P

HEAD_DIM = 128
LANES = 128


beta_first = 0.9
beta_second = 0.999
learning_rate = 0.1
weight_decay = 0.1
epsilon = 1e-08
step_count = 10.0


def adamw(master, moment, second, gradient):
    moment_new = beta_first * moment + (1.0 - beta_first) * gradient
    second_new = beta_second * second + (1.0 - beta_second) * gradient * gradient
    moment_hat = moment_new / (1.0 - beta_first**step_count)
    second_hat = second_new / (1.0 - beta_second**step_count)
    return master - learning_rate * (
        moment_hat / (jnp.sqrt(second_hat) + epsilon) + weight_decay * master
    )


def swap(array, axis, count, distance):
    return lax.ppermute(array, axis, [(i, i ^ distance) for i in range(count)])


SMEM = pl.BlockSpec(memory_space=pltpu.SMEM)
VMEM = pl.BlockSpec(memory_space=pltpu.VMEM)
HBM = pl.BlockSpec(memory_space=pltpu.HBM)
PARAMS = pltpu.CompilerParams(vmem_limit_bytes=32 * 1024 * 1024)


def in_hbm(array):
    return pltpu.with_memory_space_constraint(array, pltpu.HBM)


def like(shape, array):
    return jax.ShapeDtypeStruct(shape, array.dtype)


def cost(moved, flops=0, transcendentals=0):
    return pl.CostEstimate(
        flops=flops, bytes_accessed=moved, transcendentals=transcendentals
    )


def pack_kernel(me_ref, queries, keys, values, *refs):
    parts, sems = refs[:-1], refs[-1]
    chips = len(parts) // 2
    width = parts[0].shape[1]
    copies = []
    for which, array in enumerate((keys, values, queries)):
        for distance in range(chips):
            chip = (me_ref[0] // 2) ^ distance
            at = pl.ds(pl.multiple_of(chip * width, width), width)
            part = parts[distance] if which == 2 else parts[chips + distance].at[which]
            sem = sems.at[which * chips + distance]
            copies.append(pltpu.make_async_copy(array.at[0, :, at], part, sem))
    for copy in copies:
        copy.start()
    for copy in copies:
        copy.wait()


def pack(me, queries, keys, values, chips):
    _, rows, features = queries.shape
    width = features // chips
    parts = pl.pallas_call(
        pack_kernel,
        out_shape=[like((rows, width), queries)] * chips
        + [like((2, rows, width), queries)] * chips,
        in_specs=[SMEM] + [HBM] * 3,
        out_specs=[VMEM] * (2 * chips),
        scratch_shapes=[pltpu.SemaphoreType.DMA((3 * chips,))],
        compiler_params=PARAMS,
        cost_estimate=cost(12 * rows * features),
        name="pack",
    )(me, *map(in_hbm, (queries, keys, values)))
    return parts[:chips], parts[chips:]


def update_kernel(*refs):
    arrays, (new_master, weight), held, sems = refs[:4], refs[4:6], refs[6], refs[7]
    copies = [
        pltpu.make_async_copy(array, held.at[index], sems.at[index])
        for index, array in enumerate(arrays)
    ]
    for copy in copies:
        copy.start()
    for copy in copies:
        copy.wait()
    result = adamw(held[0], held[1], held[2], held[3])
    new_master[...] = result
    weight[...] = result.astype(weight.dtype)


def update(*arrays):
    shape, kind = arrays[0].shape, arrays[0].dtype
    return pl.pallas_call(
        update_kernel,
        out_shape=[like(shape, arrays[0]), jax.ShapeDtypeStruct(shape, jnp.bfloat16)],
        in_specs=[HBM] * 4,
        out_specs=[VMEM] * 2,
        scratch_shapes=[pltpu.VMEM((4, *shape), kind), pltpu.SemaphoreType.DMA((4,))],
        compiler_params=PARAMS,
        cost_estimate=cost(22 * arrays[0].size),
        name="update",
    )(*map(in_hbm, arrays))


def merge_kernel(index_ref, *refs):
    pieces, whole = refs[:-1], refs[-1]
    for distance, piece in enumerate(pieces):
        whole[:, index_ref[0] ^ distance] = piece[...]


def merge(index, pieces):
    shape = (pieces[0].shape[0], len(pieces)) + pieces[0].shape[1:]
    return pl.pallas_call(
        merge_kernel,
        out_shape=like(shape, pieces[0]),
        in_specs=[SMEM] + [VMEM] * len(pieces),
        out_specs=VMEM,
        compiler_params=PARAMS,
        cost_estimate=cost(4 * len(pieces) * pieces[0].size),
        name="merge",
    )(index, *pieces)


def stack_kernel(*refs):
    pieces, stacked = refs[:-1], refs[-1]
    for index, piece in enumerate(pieces):
        stacked[index] = piece[...]


def stack(pieces):
    return pl.pallas_call(
        stack_kernel,
        out_shape=like((len(pieces), *pieces[0].shape), pieces[0]),
        in_specs=[VMEM] * len(pieces),
        out_specs=VMEM,
        compiler_params=PARAMS,
        cost_estimate=cost(4 * len(pieces) * pieces[0].size),
        name="stack",
    )(*pieces)


def gather_kernel(me_ref, own, other, keys, values):
    chips, _, rows, _ = own.shape
    heads, length, _ = values.shape
    for head in range(heads):
        values[head, :, HEAD_DIM:] = jnp.ones((length, LANES), values.dtype)
    for distance in range(chips):
        for core, pair in enumerate((own, other)):
            block = me_ref[0] ^ (2 * distance + core)
            at = pl.ds(pl.multiple_of(block * rows, rows), rows)
            keys[at, :] = pair[distance, 0]
            for head in range(heads):
                values[head, at, :HEAD_DIM] = pair[
                    distance, 1, :, head * HEAD_DIM : (head + 1) * HEAD_DIM
                ]


def gather(me, own, other):
    chips, _, rows, width = own.shape
    length = 2 * chips * rows
    return pl.pallas_call(
        gather_kernel,
        out_shape=[
            like((length, width), own),
            like((width // HEAD_DIM, length, HEAD_DIM + LANES), own),
        ],
        in_specs=[SMEM] + [VMEM] * 2,
        out_specs=[VMEM] * 2,
        compiler_params=PARAMS,
        cost_estimate=cost(10 * length * width),
        name="gather",
    )(me, own, other)


def attend_kernel(distances, me_ref, *refs):
    many = len(distances)
    parts, (keys, values, attended, queries, result) = refs[:many], refs[many:]
    rows, width = parts[0].shape
    near = 2 * rows
    half = width // 2
    chip, core = me_ref[0] // 2, me_ref[0] % 2
    scale = HEAD_DIM ** (-0.5) * math.log2(math.e)

    def attend_from(here):
        chips = sorted(here ^ distance for distance in distances)
        place = {chip: index * rows for index, chip in enumerate(chips)}
        for distance, part in zip(distances, parts):
            at = place[here ^ distance]
            queries[at : at + rows, :] = part[...]
        causal = core * rows + lax.broadcasted_iota(
            jnp.int32, (rows, near), 0
        ) >= lax.broadcasted_iota(jnp.int32, (rows, near), 1)
        for head in range(width // HEAD_DIM):
            columns = slice(head * HEAD_DIM, (head + 1) * HEAD_DIM)
            tiles = []
            for c in range(chips[-1] + 1):
                first = min(place[chip] for chip in chips if chip >= c)
                score = lax.dot_general(
                    queries[first : many * rows, columns],
                    keys[c * near : (c + 1) * near, columns],
                    (((1,), (1,)), ((), ())),
                    preferred_element_type=jnp.float32,
                )
                if c in place:
                    masked = jnp.where(causal, score[:rows], -jnp.inf)
                    later = [score[rows:]] if first + rows < many * rows else []
                    score = jnp.concatenate([masked, *later], axis=0)
                tiles.append((c, first, score))
            highest = []
            for chip in chips:
                best = None
                for c, first, score in tiles:
                    if c <= chip:
                        at = place[chip] - first
                        block = score[at : at + rows]
                        best = block if best is None else jnp.maximum(best, block)
                highest.append(jnp.max(best, axis=1, keepdims=True))
            highest = jnp.concatenate(highest, axis=0)
            totals, start = None, 0
            for c, first, score in tiles:
                expons = jnp.exp2((score - highest[first:]) * scale).astype(jnp.bfloat16)
                total = jnp.dot(
                    expons,
                    values[head, c * near : (c + 1) * near],
                    preferred_element_type=jnp.float32,
                )
                totals = total if totals is None else totals[first - start :] + total
                start = first
                if c in place:
                    result[first : first + rows, columns] = (
                        totals[:rows, :HEAD_DIM] / totals[:rows, HEAD_DIM:]
                    ).astype(result.dtype)
        for index, distance in enumerate(distances):
            at = place[here ^ distance]
            for part in range(2):
                attended[part, index * rows : (index + 1) * rows, :] = result[
                    at : at + rows, part * half : (part + 1) * half
                ]

    for here in range(keys.shape[0] // near):
        pl.when(chip == here)(functools.partial(attend_from, here))


def attend(me, distances, parts, keys, values):
    rows, width = parts[0].shape
    length = keys.shape[0]
    total = len(parts) * rows
    return pl.pallas_call(
        functools.partial(attend_kernel, distances),
        out_shape=like((2, total, width // 2), keys),
        in_specs=[SMEM] + [VMEM] * (len(parts) + 2),
        out_specs=VMEM,
        scratch_shapes=[pltpu.VMEM((total, width), keys.dtype)] * 2,
        compiler_params=PARAMS,
        cost_estimate=cost(
            6 * length * width + 4 * total * width,
            4 * total * length * width,
            total * length * (width // HEAD_DIM),
        ),
        name="attend",
    )(me, *parts, keys, values)


def project_kernel(me_ref, attended, own_weight, their_weight, *outs):
    core = me_ref[0] % 2
    product = jnp.dot(attended[core], own_weight[...], preferred_element_type=jnp.float32)
    product += jnp.dot(attended[1 - core], their_weight[...], preferred_element_type=jnp.float32)
    rows, columns = outs[0].shape
    across = product.shape[1] // columns
    for index, out in enumerate(outs):
        down, right = index // across * rows, index % across * columns
        out[...] = product[down : down + rows, right : right + columns].astype(out.dtype)


def project(me, attended, own_weight, their_weight, shape, kind):
    _, total, features = attended.shape
    width = own_weight.shape[1]
    many = total * width // math.prod(shape)
    return pl.pallas_call(
        project_kernel,
        out_shape=[jax.ShapeDtypeStruct(shape, kind)] * many,
        in_specs=[SMEM] + [VMEM] * 3,
        out_specs=[VMEM] * many,
        compiler_params=PARAMS,
        cost_estimate=cost(
            4 * total * features + 4 * features * width + 4 * total * width,
            4 * total * features * width,
        ),
        name="project",
    )(me, attended, own_weight, their_weight)


def add_kernel(marks, *refs):
    products, (left, right), outs = refs[: len(marks)], refs[len(marks) : -len(marks)], refs[-len(marks) :]
    half = left.shape[1]
    for mark, product, out in zip(marks, products, outs):
        out[...] = product[...].astype(out.dtype)
        if mark == 1:
            out[:, :half] = (product[:, :half] + left[...].astype(jnp.float32)).astype(out.dtype)
        if mark == 2:
            out[:, half:] = (product[:, half:] + right[...].astype(jnp.float32)).astype(out.dtype)


def add(marks, products, left, right):
    return pl.pallas_call(
        functools.partial(add_kernel, marks),
        out_shape=[like(product.shape, left) for product in products],
        in_specs=[VMEM] * (len(products) + 2),
        out_specs=[VMEM] * len(products),
        compiler_params=PARAMS,
        cost_estimate=cost(8 * len(products) * products[0].size),
        name="add",
    )(*products, left, right)


def make_body(seq_count, dp_count):
    chips = seq_count // 2

    def body(queries, keys, values, master, moment, second, gradient):
        own_features = queries.shape[2] // seq_count
        out_features = master.shape[1]
        me = lax.axis_index("seq").astype(jnp.int32).reshape(1)
        place = lax.axis_index("dp").astype(jnp.int32)

        query_parts, pair_parts = pack(me, queries, keys, values, chips)
        pairs = [pair_parts[0]]
        pairs += [swap(pair_parts[d], "seq", seq_count, 2 * d) for d in range(1, chips)]

        state, _ = lax.optimization_barrier(((master, moment, second, gradient), pair_parts))
        new_master, weight = update(*state)
        weight = weight[None]
        span = dp_count
        while span > 1:
            many = 4 if span % 4 == 0 else 2
            span //= many
            pieces = [weight, swap(weight, "dp", dp_count, span)]
            if many == 4:
                pieces.append(swap(weight, "dp", dp_count, 2 * span))
            if span == 1:
                pairs, pieces = lax.optimization_barrier((pairs, pieces))
            if many == 4:
                pieces.append(swap(pieces[2], "dp", dp_count, span))
            if span > 1:
                weight = merge((place // span % many).reshape(1), pieces)
                weight = weight.reshape(-1, *weight.shape[2:])
        own_pairs = stack(pairs)
        other_pairs = swap(own_pairs, "seq", seq_count, 1)
        sent, _ = lax.optimization_barrier((query_parts[1:], pairs))
        own_queries = [query_parts[0]]
        own_queries += [swap(part, "seq", seq_count, 2 * d) for d, part in enumerate(sent, 1)]
        own_queries, other_pairs = lax.optimization_barrier((own_queries, other_pairs))
        all_keys, all_values = gather(me, own_pairs, other_pairs)
        pieces, all_keys = lax.optimization_barrier((pieces, all_keys))
        weight = merge((place % len(pieces)).reshape(1), pieces)
        own_weight = weight.reshape(own_features, out_features)
        their_weight = swap(own_weight, "seq", seq_count, 1)

        rows = queries.shape[1]
        far = chips - 1
        attended = attend(me, (far,), [own_queries[far]], all_keys, all_values)
        halves = project(
            me, attended, own_weight, their_weight, (rows, out_features // 2), attended.dtype
        )
        left = swap(halves[0], "seq", seq_count, 2)
        right = swap(halves[1], "seq", seq_count, 4)
        near = tuple(range(far))
        attended = attend(me, near, own_queries[:far], all_keys, all_values)
        projected, *products = project(
            me, attended, own_weight, their_weight, (rows, out_features), jnp.float32
        )
        marks = [{far ^ 1: 1, far ^ 2: 2}.get(d, 0) for d in near[1:]]
        sent = add(marks, products, left, right)
        for d, block in zip(near[1:], sent):
            projected += swap(block, "seq", seq_count, 2 * d).astype(jnp.float32)
        projected = projected.astype(jnp.bfloat16)[None]
        return (projected, new_master)

    return body


def solution(mesh):
    tokens = P("dp", "seq", None)
    rows = P(("seq", "dp"), None)
    return jax.shard_map(
        make_body(mesh.shape["seq"], mesh.shape["dp"]),
        mesh=mesh,
        in_specs=(tokens,) * 3 + (rows,) * 4,
        out_specs=(tokens, rows),
        check_vma=False,
    )
```

```python
import functools
import math

import jax
import jax.numpy as jnp
from jax import lax
from jax.experimental import pallas as pl
from jax.experimental.pallas import tpu as pltpu
from jax.sharding import PartitionSpec as P

HEAD_DIM = 128
LANES = 128


beta_first = 0.9
beta_second = 0.999
learning_rate = 0.1
weight_decay = 0.1
epsilon = 1e-08
step_count = 10.0


def adamw(master, moment, second, gradient):
    moment_new = beta_first * moment + (1.0 - beta_first) * gradient
    second_new = beta_second * second + (1.0 - beta_second) * gradient * gradient
    moment_hat = moment_new / (1.0 - beta_first**step_count)
    second_hat = second_new / (1.0 - beta_second**step_count)
    return master - learning_rate * (
        moment_hat / (jnp.sqrt(second_hat) + epsilon) + weight_decay * master
    )


def swap(array, axis, count, distance):
    return lax.ppermute(array, axis, [(i, i ^ distance) for i in range(count)])


SMEM = pl.BlockSpec(memory_space=pltpu.SMEM)
VMEM = pl.BlockSpec(memory_space=pltpu.VMEM)
HBM = pl.BlockSpec(memory_space=pltpu.HBM)
PARAMS = pltpu.CompilerParams(vmem_limit_bytes=14 * 1024 * 1024)


def in_hbm(array):
    return pltpu.with_memory_space_constraint(array, pltpu.HBM)


def like(shape, array):
    return jax.ShapeDtypeStruct(shape, array.dtype)


def cost(moved, flops=0, transcendentals=0):
    return pl.CostEstimate(
        flops=flops, bytes_accessed=moved, transcendentals=transcendentals
    )


def chip_columns(me_ref, distance, width):
    return pl.ds(pl.multiple_of(((me_ref[0] // 2) ^ distance) * width, width), width)


def pack_kernel(me_ref, keys, values, queries, *refs):
    pairs, (here, sems) = refs[:-2], refs[-2:]
    width = here.shape[1]
    copies = []

    def copy(array, distance, part):
        at = chip_columns(me_ref, distance, width)
        copies.append(pltpu.make_async_copy(array.at[0, :, at], part, sems.at[len(copies)]))
        copies[-1].start()

    for distance, pair in enumerate(pairs):
        copy(keys, distance, pair.at[0])
        copy(values, distance, pair.at[1])
    copy(queries, 0, here)
    for each in copies:
        each.wait()


def pack(me, keys, values, queries, chips):
    _, rows, features = queries.shape
    width = features // chips
    *pairs, here = pl.pallas_call(
        pack_kernel,
        out_shape=[like((2, rows, width), queries)] * chips + [like((rows, width), queries)],
        in_specs=[SMEM] + [HBM] * 3,
        out_specs=[VMEM] * (chips + 1),
        scratch_shapes=[pltpu.SemaphoreType.DMA((2 * chips + 1,))],
        compiler_params=PARAMS,
        cost_estimate=cost(8 * rows * features),
        name="pack",
    )(me, *map(in_hbm, (keys, values, queries)))
    return pairs, here


def pack_queries_kernel(me_ref, queries, *refs):
    many = len(refs) - 2
    parts, (held, sems) = refs[:-2], refs[-2:]
    width = held.shape[2]
    arrive = [
        pltpu.make_async_copy(
            queries.at[0, :, chip_columns(me_ref, index + 1, width)],
            held.at[index],
            sems.at[index],
        )
        for index in range(many)
    ]
    leave = [
        pltpu.make_async_copy(held.at[index], part, sems.at[index])
        for index, part in enumerate(parts)
    ]
    for copy in arrive:
        copy.start()
    for first, second in zip(arrive, leave):
        first.wait()
        second.start()
    for copy in leave:
        copy.wait()


def pack_queries(me, queries, chips):
    _, rows, features = queries.shape
    width, many = features // chips, chips - 1
    return pl.pallas_call(
        pack_queries_kernel,
        out_shape=[pltpu.HBM((rows, width), queries.dtype)] * many,
        in_specs=[SMEM, HBM],
        out_specs=[HBM] * many,
        scratch_shapes=[
            pltpu.VMEM((many, rows, width), queries.dtype),
            pltpu.SemaphoreType.DMA((many,)),
        ],
        compiler_params=PARAMS,
        cost_estimate=cost(4 * rows * features),
        name="pack_queries",
    )(me, in_hbm(queries))


def weigh_kernel(*refs):
    arrays, weight, held, sems = refs[:4], refs[4], refs[5], refs[6]
    pieces = sems.shape[1]
    rows = weight.shape[0] // pieces
    copies = []
    for piece in range(pieces):
        at = pl.ds(piece * rows, rows)
        copies.append(
            [
                pltpu.make_async_copy(array.at[at], held.at[index, at], sems.at[index, piece])
                for index, array in enumerate(arrays)
            ]
        )
        for copy in copies[-1]:
            copy.start()
    for piece in range(pieces):
        for copy in copies[piece]:
            copy.wait()
        at = pl.ds(piece * rows, rows)
        result = adamw(held[0, at], held[1, at], held[2, at], held[3, at])
        weight[at, :] = result.astype(weight.dtype)


def weigh(*arrays):
    shape, kind = arrays[0].shape, arrays[0].dtype
    pieces = math.gcd(shape[0] // 16, 4) if shape[0] % 16 == 0 else 1
    return pl.pallas_call(
        weigh_kernel,
        out_shape=jax.ShapeDtypeStruct(shape, jnp.bfloat16),
        in_specs=[HBM] * 4,
        out_specs=VMEM,
        scratch_shapes=[pltpu.VMEM((4, *shape), kind), pltpu.SemaphoreType.DMA((4, pieces))],
        compiler_params=PARAMS,
        cost_estimate=cost(18 * arrays[0].size),
        name="weigh",
    )(*map(in_hbm, arrays))


def merge_kernel(index_ref, *refs):
    pieces, whole = refs[:-1], refs[-1]
    for distance, piece in enumerate(pieces):
        whole[index_ref[0] ^ distance] = piece[...]


def merge(index, pieces):
    return pl.pallas_call(
        merge_kernel,
        out_shape=like((len(pieces), *pieces[0].shape), pieces[0]),
        in_specs=[SMEM] + [VMEM] * len(pieces),
        out_specs=VMEM,
        compiler_params=PARAMS,
        cost_estimate=cost(4 * len(pieces) * pieces[0].size),
        name="merge",
    )(index, *pieces)


def places(chips, rows, pieces, width):
    tokens = [slice(index * rows, (index + 1) * rows) for index in range(2 * chips)]
    down, out_features = pieces.shape
    first, across = 2 * chips * rows, out_features // width
    weights = [
        slice(first + index * down, first + (index + 1) * down) for index in range(3 * across)
    ]
    return tokens, [weights[index * across : (index + 1) * across] for index in range(3)]


def stack_kernel(chips, *refs):
    pairs, pieces, stacked = refs[:chips], refs[chips:-1], refs[-1]
    rows, width = pairs[0].shape[1:]
    tokens, weights = places(chips, rows, pieces[0], width)
    for distance, pair in enumerate(pairs):
        stacked[tokens[2 * distance], :] = pair[0]
        stacked[tokens[2 * distance + 1], :] = pair[1]
    for piece, blocks in zip(pieces, weights):
        for index, block in enumerate(blocks):
            stacked[block, :] = piece[:, index * width : (index + 1) * width]


def stack(pairs, pieces):
    chips = len(pairs)
    _, rows, width = pairs[0].shape
    total = 2 * chips * rows + len(pieces) * pieces[0].size // width
    return pl.pallas_call(
        functools.partial(stack_kernel, chips),
        out_shape=like((total, width), pairs[0]),
        in_specs=[VMEM] * (chips + len(pieces)),
        out_specs=VMEM,
        compiler_params=PARAMS,
        cost_estimate=cost(4 * total * width),
        name="stack",
    )(*pairs, *pieces)


def weights_kernel(chips, rows, index_ref, own, own_last, other, other_last, weights):
    down, out_features = own_last.shape
    width = own.shape[1]
    _, blocks = places(chips, rows, own_last, width)
    for which, (stacked, last) in enumerate(((own, own_last), (other, other_last))):
        for distance in range(4):
            at = pl.ds(pl.multiple_of((index_ref[0] ^ distance) * down, down), down)
            if distance == 3:
                weights[which, at, :] = last[...]
            else:
                for index, block in enumerate(blocks[distance]):
                    weights[which, at, index * width : (index + 1) * width] = stacked[block, :]


def collect(index, chips, rows, own, own_last, other, other_last):
    down, out_features = own_last.shape
    shape = (2, 4 * down, out_features)
    return pl.pallas_call(
        functools.partial(weights_kernel, chips, rows),
        out_shape=like(shape, own),
        in_specs=[SMEM] + [VMEM] * 4,
        out_specs=VMEM,
        compiler_params=PARAMS,
        cost_estimate=cost(4 * math.prod(shape)),
        name="collect",
    )(index, own, own_last, other, other_last)


def attend_kernel(distances, chips, me_ref, *refs):
    many = len(distances)
    parts, (own, other, attended, queries, result) = refs[:many], refs[many:]
    total, width = queries.shape
    rows = total // many
    half = width // 2
    chip, core = me_ref[0] // 2, me_ref[0] % 2
    scale = HEAD_DIM ** (-0.5) * math.log2(math.e)

    def attend_from(here):
        order = sorted(here ^ distance for distance in distances)
        place = {chip: index * rows for index, chip in enumerate(order)}
        for distance, part in zip(distances, parts):
            at = place[here ^ distance]
            queries[at : at + rows, :] = part[...]
        row = lax.broadcasted_iota(jnp.int32, (rows, 2 * rows), 0)
        column = lax.broadcasted_iota(jnp.int32, (rows, 2 * rows), 1)
        causal = jnp.where(column < rows, row, 2 * rows * core - 1) >= column

        def both(index, columns):
            at = slice(index * rows, (index + 1) * rows)
            return jnp.concatenate([own[at, columns], other[at, columns]], axis=0)

        ones = jnp.ones((2 * rows, LANES), own.dtype)
        for head in range(width // HEAD_DIM):
            columns = slice(head * HEAD_DIM, (head + 1) * HEAD_DIM)
            tiles = []
            for c in range(order[-1] + 1):
                first = min(place[chip] for chip in order if chip >= c)
                score = lax.dot_general(
                    queries[first : many * rows, columns],
                    both(2 * (here ^ c), columns),
                    (((1,), (1,)), ((), ())),
                    preferred_element_type=jnp.float32,
                )
                if c in place:
                    masked = jnp.where(causal, score[:rows], -jnp.inf)
                    later = [score[rows:]] if first + rows < many * rows else []
                    score = jnp.concatenate([masked, *later], axis=0)
                tiles.append((c, first, score))
            highest = []
            for chip in order:
                best = None
                for c, first, score in tiles:
                    if c <= chip:
                        at = place[chip] - first
                        block = score[at : at + rows]
                        best = block if best is None else jnp.maximum(best, block)
                highest.append(jnp.max(best, axis=1, keepdims=True))
            highest = jnp.concatenate(highest, axis=0)
            totals, start = None, 0
            for c, first, score in tiles:
                expons = jnp.exp2((score - highest[first:]) * scale).astype(jnp.bfloat16)
                seen = jnp.concatenate([both(2 * (here ^ c) + 1, columns), ones], axis=1)
                total = jnp.dot(expons, seen, preferred_element_type=jnp.float32)
                totals = total if totals is None else totals[first - start :] + total
                start = first
                if c in place:
                    result[first : first + rows, columns] = (
                        totals[:rows, :HEAD_DIM] / totals[:rows, HEAD_DIM:]
                    ).astype(result.dtype)
        for index, distance in enumerate(distances):
            at = place[here ^ distance]
            for part in range(2):
                attended[part, index * rows : (index + 1) * rows, :] = result[
                    at : at + rows, part * half : (part + 1) * half
                ]

    for here in range(chips):
        pl.when(chip == here)(functools.partial(attend_from, here))


def attend(me, distances, parts, own, other, chips):
    rows, width = parts[0].shape[-2:]
    length = 2 * chips * rows
    total = len(parts) * rows
    return pl.pallas_call(
        functools.partial(attend_kernel, distances, chips),
        out_shape=like((2, total, width // 2), own),
        in_specs=[SMEM] + [VMEM] * (len(parts) + 2),
        out_specs=VMEM,
        scratch_shapes=[pltpu.VMEM((total, width), own.dtype)] * 2,
        compiler_params=PARAMS,
        cost_estimate=cost(
            4 * length * width + 4 * total * width,
            4 * total * length * width,
            total * length * (width // HEAD_DIM),
        ),
        name="attend",
    )(me, *parts, own, other)


def project_kernel(me_ref, attended, weights, *outs):
    core = me_ref[0] % 2
    product = jnp.dot(attended[core], weights[0], preferred_element_type=jnp.float32)
    product += jnp.dot(attended[1 - core], weights[1], preferred_element_type=jnp.float32)
    rows, columns = outs[0].shape
    across = product.shape[1] // columns
    for index, out in enumerate(outs):
        down, right = index // across * rows, index % across * columns
        out[...] = product[down : down + rows, right : right + columns].astype(out.dtype)


def project(me, attended, weights, shape, kind):
    _, total, features = attended.shape
    width = weights.shape[2]
    many = total * width // math.prod(shape)
    return pl.pallas_call(
        project_kernel,
        out_shape=[jax.ShapeDtypeStruct(shape, kind)] * many,
        in_specs=[SMEM] + [VMEM] * 2,
        out_specs=[VMEM] * many,
        compiler_params=PARAMS,
        cost_estimate=cost(
            4 * total * features + 4 * features * width + 4 * total * width,
            4 * total * features * width,
        ),
        name="project",
    )(me, attended, weights)


def add_kernel(marks, *refs):
    products, (left, right), outs = refs[: len(marks)], refs[len(marks) : -len(marks)], refs[-len(marks) :]
    half = left.shape[1]
    for mark, product, out in zip(marks, products, outs):
        out[...] = product[...].astype(out.dtype)
        if mark == 1:
            out[:, :half] = (product[:, :half] + left[...].astype(jnp.float32)).astype(out.dtype)
        if mark == 2:
            out[:, half:] = (product[:, half:] + right[...].astype(jnp.float32)).astype(out.dtype)


def add(marks, products, left, right):
    return pl.pallas_call(
        functools.partial(add_kernel, marks),
        out_shape=[like(product.shape, left) for product in products],
        in_specs=[VMEM] * (len(products) + 2),
        out_specs=[VMEM] * len(products),
        compiler_params=PARAMS,
        cost_estimate=cost(8 * len(products) * products[0].size),
        name="add",
    )(*products, left, right)


def make_body(seq_count, dp_count):
    chips = seq_count // 2
    far = chips - 1

    def to_chip(part, distance):
        return swap(part, "seq", seq_count, 2 * distance)

    def exchange(parts):
        got = [to_chip(part, d) if d else part for d, part in enumerate(parts)]
        return [*got[:-1], lax.optimization_barrier(got[-1])]

    def body(queries, keys, values, master, moment, second, gradient):
        rows = queries.shape[1]
        out_features = master.shape[1]
        me = lax.axis_index("seq").astype(jnp.int32).reshape(1)
        place = lax.axis_index("dp").astype(jnp.int32)

        sent_pairs, own_queries = pack(me, keys, values, queries, chips)
        pairs = exchange(sent_pairs)

        state, _ = lax.optimization_barrier(((master, moment, second, gradient), sent_pairs))
        weight = weigh(*state)[None]
        span = 1
        while 4 * span < dp_count:
            many = 4 if dp_count // span % 16 == 0 else 2
            pieces = [weight] + [swap(weight, "dp", dp_count, span * d) for d in range(1, many)]
            weight = merge((place // span % many).reshape(1), pieces)
            weight = weight.reshape(-1, *weight.shape[2:])
            span *= many
        weight = weight.reshape(-1, out_features)
        pieces = [weight] + [swap(weight, "dp", dp_count, span * d) for d in (1, 2)]
        queries, _ = lax.optimization_barrier((queries, weight))
        sent_queries = pack_queries(me, queries, chips)
        pairs, sent_queries = lax.optimization_barrier((pairs, sent_queries))
        own = stack(pairs, pieces)
        forwarded = swap(pieces[2], "dp", dp_count, span)

        other = swap(own, "seq", seq_count, 1)
        sent_queries, _ = lax.optimization_barrier((sent_queries, own))
        own_queries = exchange([own_queries, *sent_queries])

        attended = attend(me, (far,), own_queries[far:], own, other, chips)
        near_queries, others, attended = lax.optimization_barrier(
            (own_queries[:far], swap(forwarded, "seq", seq_count, 1), attended)
        )
        index = (place // span % 4).reshape(1)
        weights = collect(index, chips, rows, own, forwarded, other, others)
        halves = project(me, attended, weights, (rows, out_features // 2), attended.dtype)
        left, right = to_chip(halves[0], 1), to_chip(halves[1], 2)
        near = tuple(range(far))
        attended = attend(me, near, near_queries, own, other, chips)
        projected, *products = project(me, attended, weights, (rows, out_features), jnp.float32)
        marks = [{far ^ 1: 1, far ^ 2: 2}.get(d, 0) for d in near[1:]]
        sent = add(marks, products, left, right)
        for d, block in zip(near[1:], sent):
            projected += to_chip(block, d).astype(jnp.float32)
        projected = projected.astype(jnp.bfloat16)[None]
        return (projected, adamw(master, moment, second, gradient))

    return body


def solution(mesh):
    tokens = P("dp", "seq", None)
    rows = P(("seq", "dp"), None)
    return jax.shard_map(
        make_body(mesh.shape["seq"], mesh.shape["dp"]),
        mesh=mesh,
        in_specs=(tokens,) * 3 + (rows,) * 4,
        out_specs=(tokens, rows),
        check_vma=False,
    )
```

```python
import functools
import math

import jax
import jax.numpy as jnp
from jax import lax
from jax.experimental import pallas as pl
from jax.experimental.pallas import tpu as pltpu
from jax.sharding import PartitionSpec as P

HEAD_DIM = 128
LANES = 128


beta_first = 0.9
beta_second = 0.999
learning_rate = 0.1
weight_decay = 0.1
epsilon = 1e-08
step_count = 10.0


def adamw(master, moment, second, gradient):
    moment_new = beta_first * moment + (1.0 - beta_first) * gradient
    second_new = beta_second * second + (1.0 - beta_second) * gradient * gradient
    moment_hat = moment_new / (1.0 - beta_first**step_count)
    second_hat = second_new / (1.0 - beta_second**step_count)
    return master - learning_rate * (
        moment_hat / (jnp.sqrt(second_hat) + epsilon) + weight_decay * master
    )


def swap(array, axis, count, distance):
    return lax.ppermute(array, axis, [(i, i ^ distance) for i in range(count)])


SMEM = pl.BlockSpec(memory_space=pltpu.SMEM)
VMEM = pl.BlockSpec(memory_space=pltpu.VMEM)
HBM = pl.BlockSpec(memory_space=pltpu.HBM)
PARAMS = pltpu.CompilerParams(vmem_limit_bytes=14 * 1024 * 1024)


def in_hbm(array):
    return pltpu.with_memory_space_constraint(array, pltpu.HBM)


def like(shape, array):
    return jax.ShapeDtypeStruct(shape, array.dtype)


def cost(moved, flops=0, transcendentals=0):
    return pl.CostEstimate(
        flops=flops, bytes_accessed=moved, transcendentals=transcendentals
    )


def chip_columns(me_ref, distance, width):
    return pl.ds(pl.multiple_of(((me_ref[0] // 2) ^ distance) * width, width), width)


def pack_kernel(me_ref, keys, values, queries, *refs):
    pairs, (here, sems) = refs[:-2], refs[-2:]
    width = here.shape[1]
    copies = []

    def copy(array, distance, part):
        at = chip_columns(me_ref, distance, width)
        copies.append(pltpu.make_async_copy(array.at[0, :, at], part, sems.at[len(copies)]))
        copies[-1].start()

    for distance, pair in enumerate(pairs):
        copy(keys, distance, pair.at[0])
        copy(values, distance, pair.at[1])
    copy(queries, 0, here)
    for each in copies:
        each.wait()


def pack(me, keys, values, queries, chips):
    _, rows, features = queries.shape
    width = features // chips
    *pairs, here = pl.pallas_call(
        pack_kernel,
        out_shape=[like((2, rows, width), queries)] * chips + [like((rows, width), queries)],
        in_specs=[SMEM] + [HBM] * 3,
        out_specs=[VMEM] * (chips + 1),
        scratch_shapes=[pltpu.SemaphoreType.DMA((2 * chips + 1,))],
        compiler_params=PARAMS,
        cost_estimate=cost(8 * rows * features),
        name="pack",
    )(me, *map(in_hbm, (keys, values, queries)))
    return pairs, here


def pack_queries_kernel(me_ref, queries, *refs):
    parts, sems = refs[:-1], refs[-1]
    width = parts[0].shape[1]
    copies = [
        pltpu.make_async_copy(
            queries.at[0, :, chip_columns(me_ref, distance, width)], part, sems.at[distance - 1]
        )
        for distance, part in enumerate(parts, 1)
    ]
    for copy in copies:
        copy.start()
    for copy in copies:
        copy.wait()


def pack_queries(me, queries, chips):
    _, rows, features = queries.shape
    width, many = features // chips, chips - 1
    return pl.pallas_call(
        pack_queries_kernel,
        out_shape=[like((rows, width), queries)] * many,
        in_specs=[SMEM, HBM],
        out_specs=[VMEM] * many,
        scratch_shapes=[pltpu.SemaphoreType.DMA((many,))],
        compiler_params=PARAMS,
        cost_estimate=cost(4 * rows * features),
        name="pack_queries",
    )(me, in_hbm(queries))


def weigh_kernel(*refs):
    arrays, weight, held, sems = refs[:4], refs[4], refs[5], refs[6]
    pieces = sems.shape[1]
    rows = weight.shape[0] // pieces
    copies = []
    for piece in range(pieces):
        at = pl.ds(piece * rows, rows)
        copies.append(
            [
                pltpu.make_async_copy(array.at[at], held.at[index, at], sems.at[index, piece])
                for index, array in enumerate(arrays)
            ]
        )
        for copy in copies[-1]:
            copy.start()
    for piece in range(pieces):
        for copy in copies[piece]:
            copy.wait()
        at = pl.ds(piece * rows, rows)
        result = adamw(held[0, at], held[1, at], held[2, at], held[3, at])
        weight[at, :] = result.astype(weight.dtype)


def weigh(*arrays):
    shape, kind = arrays[0].shape, arrays[0].dtype
    pieces = math.gcd(shape[0] // 16, 4) if shape[0] % 16 == 0 else 1
    return pl.pallas_call(
        weigh_kernel,
        out_shape=jax.ShapeDtypeStruct(shape, jnp.bfloat16),
        in_specs=[HBM] * 4,
        out_specs=VMEM,
        scratch_shapes=[pltpu.VMEM((4, *shape), kind), pltpu.SemaphoreType.DMA((4, pieces))],
        compiler_params=PARAMS,
        cost_estimate=cost(18 * arrays[0].size),
        name="weigh",
    )(*map(in_hbm, arrays))


def merge_kernel(index_ref, *refs):
    pieces, whole = refs[:-1], refs[-1]
    for distance, piece in enumerate(pieces):
        whole[index_ref[0] ^ distance] = piece[...]


def merge(index, pieces):
    return pl.pallas_call(
        merge_kernel,
        out_shape=like((len(pieces), *pieces[0].shape), pieces[0]),
        in_specs=[SMEM] + [VMEM] * len(pieces),
        out_specs=VMEM,
        compiler_params=PARAMS,
        cost_estimate=cost(4 * len(pieces) * pieces[0].size),
        name="merge",
    )(index, *pieces)


def places(chips, rows, pieces, width):
    tokens = [slice(index * rows, (index + 1) * rows) for index in range(2 * chips)]
    down, out_features = pieces.shape
    first, across = 2 * chips * rows, out_features // width
    weights = [
        slice(first + index * down, first + (index + 1) * down) for index in range(3 * across)
    ]
    return tokens, [weights[index * across : (index + 1) * across] for index in range(3)]


def stack_kernel(chips, *refs):
    pairs, pieces, stacked = refs[:chips], refs[chips:-1], refs[-1]
    rows, width = pairs[0].shape[1:]
    tokens, weights = places(chips, rows, pieces[0], width)
    for distance, pair in enumerate(pairs):
        stacked[tokens[2 * distance], :] = pair[0]
        stacked[tokens[2 * distance + 1], :] = pair[1]
    for piece, blocks in zip(pieces, weights):
        for index, block in enumerate(blocks):
            stacked[block, :] = piece[:, index * width : (index + 1) * width]


def stack(pairs, pieces):
    chips = len(pairs)
    _, rows, width = pairs[0].shape
    total = 2 * chips * rows + len(pieces) * pieces[0].size // width
    return pl.pallas_call(
        functools.partial(stack_kernel, chips),
        out_shape=like((total, width), pairs[0]),
        in_specs=[VMEM] * (chips + len(pieces)),
        out_specs=VMEM,
        compiler_params=PARAMS,
        cost_estimate=cost(4 * total * width),
        name="stack",
    )(*pairs, *pieces)


def collect_kernel(chips, rows, index_ref, own, last, other, weights):
    down, out_features = last.shape
    width = own.shape[1]
    _, blocks = places(chips, rows, last, width)
    for which, stacked in enumerate((own, other)):
        for distance in range(3):
            at = pl.ds(pl.multiple_of((index_ref[0] ^ distance) * down, down), down)
            for index, block in enumerate(blocks[distance]):
                weights[which, at, index * width : (index + 1) * width] = stacked[block, :]
    at = pl.ds(pl.multiple_of((index_ref[0] ^ 3) * down, down), down)
    weights[0, at, :] = last[...]
    weights[1, at, :] = jnp.zeros_like(last)


def collect(index, chips, rows, own, last, other):
    down, out_features = last.shape
    shape = (2, 4 * down, out_features)
    return pl.pallas_call(
        functools.partial(collect_kernel, chips, rows),
        out_shape=like(shape, own),
        in_specs=[SMEM] + [VMEM] * 3,
        out_specs=VMEM,
        compiler_params=PARAMS,
        cost_estimate=cost(4 * math.prod(shape)),
        name="collect",
    )(index, own, last, other)


def attend_kernel(distances, chips, me_ref, *refs):
    many = len(distances)
    parts, (own, other, attended, queries, result) = refs[:many], refs[many:]
    total, width = queries.shape
    rows = total // many
    half = width // 2
    chip, core = me_ref[0] // 2, me_ref[0] % 2
    scale = HEAD_DIM ** (-0.5) * math.log2(math.e)

    def attend_from(here):
        order = sorted(here ^ distance for distance in distances)
        place = {chip: index * rows for index, chip in enumerate(order)}
        for distance, part in zip(distances, parts):
            at = place[here ^ distance]
            queries[at : at + rows, :] = part[...]
        row = lax.broadcasted_iota(jnp.int32, (rows, 2 * rows), 0)
        column = lax.broadcasted_iota(jnp.int32, (rows, 2 * rows), 1)
        causal = jnp.where(column < rows, row, 2 * rows * core - 1) >= column

        def both(index, columns):
            at = slice(index * rows, (index + 1) * rows)
            return jnp.concatenate([own[at, columns], other[at, columns]], axis=0)

        ones = jnp.ones((2 * rows, LANES), own.dtype)
        for head in range(width // HEAD_DIM):
            columns = slice(head * HEAD_DIM, (head + 1) * HEAD_DIM)
            tiles = []
            for c in range(order[-1] + 1):
                first = min(place[chip] for chip in order if chip >= c)
                score = lax.dot_general(
                    queries[first : many * rows, columns],
                    both(2 * (here ^ c), columns),
                    (((1,), (1,)), ((), ())),
                    preferred_element_type=jnp.float32,
                )
                if c in place:
                    masked = jnp.where(causal, score[:rows], -jnp.inf)
                    later = [score[rows:]] if first + rows < many * rows else []
                    score = jnp.concatenate([masked, *later], axis=0)
                tiles.append((c, first, score))
            highest = []
            for chip in order:
                best = None
                for c, first, score in tiles:
                    if c <= chip:
                        at = place[chip] - first
                        block = score[at : at + rows]
                        best = block if best is None else jnp.maximum(best, block)
                highest.append(jnp.max(best, axis=1, keepdims=True))
            highest = jnp.concatenate(highest, axis=0)
            totals, start = None, 0
            for c, first, score in tiles:
                expons = jnp.exp2((score - highest[first:]) * scale).astype(jnp.bfloat16)
                seen = jnp.concatenate([both(2 * (here ^ c) + 1, columns), ones], axis=1)
                total = jnp.dot(expons, seen, preferred_element_type=jnp.float32)
                totals = total if totals is None else totals[first - start :] + total
                start = first
                if c in place:
                    result[first : first + rows, columns] = (
                        totals[:rows, :HEAD_DIM] / totals[:rows, HEAD_DIM:]
                    ).astype(result.dtype)
        for index, distance in enumerate(distances):
            at = place[here ^ distance]
            for part in range(2):
                attended[part, index * rows : (index + 1) * rows, :] = result[
                    at : at + rows, part * half : (part + 1) * half
                ]

    for here in range(chips):
        pl.when(chip == here)(functools.partial(attend_from, here))


def attend(me, distances, parts, own, other, chips):
    rows, width = parts[0].shape[-2:]
    length = 2 * chips * rows
    total = len(parts) * rows
    return pl.pallas_call(
        functools.partial(attend_kernel, distances, chips),
        out_shape=like((2, total, width // 2), own),
        in_specs=[SMEM] + [VMEM] * (len(parts) + 2),
        out_specs=VMEM,
        scratch_shapes=[pltpu.VMEM((total, width), own.dtype)] * 2,
        compiler_params=PARAMS,
        cost_estimate=cost(
            4 * length * width + 4 * total * width,
            4 * total * length * width,
            total * length * (width // HEAD_DIM),
        ),
        name="attend",
    )(me, *parts, own, other)


def project_kernel(chips, me_ref, index_ref, attended, weights, last, *refs):
    outs, other = refs[:-1], refs[-1]
    down = last.shape[0]
    core = me_ref[0] % 2
    other[...] = weights[1]
    other[pl.ds(pl.multiple_of((index_ref[0] ^ 3) * down, down), down), :] = last[...]
    product = jnp.dot(attended[core], weights[0], preferred_element_type=jnp.float32)
    product += jnp.dot(attended[1 - core], other[...], preferred_element_type=jnp.float32)
    rows = outs[0].shape[0]

    def give(out, distance):
        out[...] = product[distance * rows : (distance + 1) * rows].astype(out.dtype)

    if len(outs) == 1:
        give(outs[0], 0)
        return
    for out, distance in zip(outs[2:], (0, *straight(chips))):
        give(out, distance)
    for which in range(2):

        @pl.when(core == which)
        def _(which=which):
            give(outs[0], early(chips, which))
            give(outs[1], late(chips, which))


def via(core):
    return 1 + core


def late(chips, core):
    return chips - 1 ^ via(core)


def early(chips, core):
    return late(chips, 1 - core)


def straight(chips):
    return [d for d in range(1, chips - 1) if d not in (late(chips, 0), late(chips, 1))]


def project(me, index, attended, weights, last, chips, kinds):
    _, total, features = attended.shape
    width = weights.shape[2]
    return pl.pallas_call(
        functools.partial(project_kernel, chips),
        out_shape=[jax.ShapeDtypeStruct((total // len(kinds), width), kind) for kind in kinds],
        in_specs=[SMEM] * 2 + [VMEM] * 3,
        out_specs=[VMEM] * len(kinds),
        scratch_shapes=[pltpu.VMEM(weights.shape[1:], weights.dtype)],
        compiler_params=PARAMS,
        cost_estimate=cost(
            4 * total * features + 6 * features * width + 4 * total * width,
            4 * total * features * width,
        ),
        name="project",
    )(me, index, attended, weights, last)


def add_kernel(product, passed, out):
    out[...] = (product[...] + passed[...].astype(jnp.float32)).astype(out.dtype)


def add(product, passed):
    return pl.pallas_call(
        add_kernel,
        out_shape=like(passed.shape, passed),
        in_specs=[VMEM] * 2,
        out_specs=VMEM,
        compiler_params=PARAMS,
        cost_estimate=cost(8 * product.size),
        name="add",
    )(product, passed)


def make_body(seq_count, dp_count):
    chips = seq_count // 2
    far = chips - 1

    def by_core(part, distance):
        return lax.ppermute(
            part, "seq", [(i, i ^ 2 * distance(i % 2)) for i in range(seq_count)]
        )

    def to_chip(part, distance):
        return swap(part, "seq", seq_count, 2 * distance)

    def exchange(parts):
        got = [to_chip(part, d) if d else part for d, part in enumerate(parts)]
        return [*got[:-1], lax.optimization_barrier(got[-1])]

    def body(queries, keys, values, master, moment, second, gradient):
        rows = queries.shape[1]
        out_features = master.shape[1]
        me = lax.axis_index("seq").astype(jnp.int32).reshape(1)
        place = lax.axis_index("dp").astype(jnp.int32)

        sent_pairs, own_queries = pack(me, keys, values, queries, chips)
        pairs = exchange(sent_pairs)

        state, _ = lax.optimization_barrier(((master, moment, second, gradient), sent_pairs))
        weight = weigh(*state)[None]
        span = 1
        while 4 * span < dp_count:
            many = 4 if dp_count // span % 16 == 0 else 2
            pieces = [weight] + [swap(weight, "dp", dp_count, span * d) for d in range(1, many)]
            weight = merge((place // span % many).reshape(1), pieces)
            weight = weight.reshape(-1, *weight.shape[2:])
            span *= many
        weight = weight.reshape(-1, out_features)
        pieces = [weight] + [swap(weight, "dp", dp_count, span * d) for d in (1, 2)]
        queries, _ = lax.optimization_barrier((queries, weight))
        sent_queries = pack_queries(me, queries, chips)
        pairs, sent_queries = lax.optimization_barrier((pairs, sent_queries))
        own = stack(pairs, pieces)
        forwarded = swap(pieces[2], "dp", dp_count, span)

        other = swap(own, "seq", seq_count, 1)
        sent_queries, _ = lax.optimization_barrier((sent_queries, own))
        own_queries = exchange([own_queries, *sent_queries])

        attended = attend(me, (far,), own_queries[far:], own, other, chips)
        attended, forwarded = lax.optimization_barrier((attended, forwarded))
        near_queries, others = lax.optimization_barrier(
            (own_queries[:far], swap(forwarded, "seq", seq_count, 1))
        )
        index = (place // span % 4).reshape(1)
        weights = collect(index, chips, rows, own, forwarded, other)
        (product,) = project(me, index, attended, weights, others, chips, [attended.dtype])
        passed = by_core(product, via)
        attended = attend(me, tuple(range(far)), near_queries, own, other, chips)
        kinds = [attended.dtype, jnp.float32, jnp.float32] + [attended.dtype] * (chips - 4)
        sent, waiting, projected, *rest = project(
            me, index, attended, weights, others, chips, kinds
        )
        got = [by_core(sent, functools.partial(early, chips))]
        got += [to_chip(product, d) for d, product in zip(straight(chips), rest)]
        for product in got:
            projected += product.astype(jnp.float32)
        projected = lax.optimization_barrier(projected)
        last = by_core(add(waiting, passed), functools.partial(late, chips))
        projected += last.astype(jnp.float32)
        projected = projected.astype(jnp.bfloat16)[None]
        return (projected, adamw(master, moment, second, gradient))

    return body


def solution(mesh):
    tokens = P("dp", "seq", None)
    rows = P(("seq", "dp"), None)
    return jax.shard_map(
        make_body(mesh.shape["seq"], mesh.shape["dp"]),
        mesh=mesh,
        in_specs=(tokens,) * 3 + (rows,) * 4,
        out_specs=(tokens, rows),
        check_vma=False,
    )
```

```python
import functools
import math

import jax
import jax.numpy as jnp
from jax import lax
from jax.experimental import pallas as pl
from jax.experimental.pallas import tpu as pltpu
from jax.sharding import PartitionSpec as P

HEAD_DIM = 128
LANES = 128


beta_first = 0.9
beta_second = 0.999
learning_rate = 0.1
weight_decay = 0.1
epsilon = 1e-08
step_count = 10.0


def adamw(master, moment, second, gradient):
    moment_new = beta_first * moment + (1.0 - beta_first) * gradient
    second_new = beta_second * second + (1.0 - beta_second) * gradient * gradient
    moment_hat = moment_new / (1.0 - beta_first**step_count)
    second_hat = second_new / (1.0 - beta_second**step_count)
    return master - learning_rate * (
        moment_hat / (jnp.sqrt(second_hat) + epsilon) + weight_decay * master
    )


def swap(array, axis, count, distance):
    return lax.ppermute(array, axis, [(i, i ^ distance) for i in range(count)])


SMEM = pl.BlockSpec(memory_space=pltpu.SMEM)
VMEM = pl.BlockSpec(memory_space=pltpu.VMEM)
HBM = pl.BlockSpec(memory_space=pltpu.HBM)
PARAMS = pltpu.CompilerParams(vmem_limit_bytes=14 * 1024 * 1024)


def in_hbm(array):
    return pltpu.with_memory_space_constraint(array, pltpu.HBM)


def like(shape, array):
    return jax.ShapeDtypeStruct(shape, array.dtype)


def cost(moved, flops=0, transcendentals=0):
    return pl.CostEstimate(
        flops=flops, bytes_accessed=moved, transcendentals=transcendentals
    )


def chip_columns(me_ref, distance, width):
    return pl.ds(pl.multiple_of(((me_ref[0] // 2) ^ distance) * width, width), width)


def start_copies(copies):
    for copy in copies:
        copy.start()
    return copies


def pair_copies(me_ref, distances, keys, values, pairs, sems):
    width = pairs[0].shape[2]
    return [
        pltpu.make_async_copy(
            array.at[0, :, chip_columns(me_ref, distance, width)],
            pair.at[which],
            sems.at[2 * index + which],
        )
        for index, (distance, pair) in enumerate(zip(distances, pairs))
        for which, array in enumerate((keys, values))
    ]


def pack_far_kernel(far, me_ref, keys, values, pair, sems):
    for copy in start_copies(pair_copies(me_ref, (far,), keys, values, (pair,), sems)):
        copy.wait()


def pack_far(me, keys, values, chips):
    _, rows, features = keys.shape
    width = features // chips
    return pl.pallas_call(
        functools.partial(pack_far_kernel, chips - 1),
        out_shape=like((2, rows, width), keys),
        in_specs=[SMEM] + [HBM] * 2,
        out_specs=VMEM,
        scratch_shapes=[pltpu.SemaphoreType.DMA((2,))],
        compiler_params=PARAMS,
        cost_estimate=cost(8 * rows * width),
        name="pack_far",
    )(me, in_hbm(keys), in_hbm(values))


def pack_kernel(far, me_ref, keys, values, queries, *refs):
    state, refs = refs[:4], refs[4:]
    pairs, (here, weight, held, sems, state_sems) = refs[:far], refs[far:]
    copies = start_copies(
        pair_copies(me_ref, range(far), keys, values, pairs, sems)
        + [
            pltpu.make_async_copy(
                queries.at[0, :, chip_columns(me_ref, 0, here.shape[1])], here, sems.at[2 * far]
            )
        ]
    )
    pieces = state_sems.shape[1]
    rows = weight.shape[0] // pieces
    places = [pl.ds(piece * rows, rows) for piece in range(pieces)]
    arriving = [
        start_copies(
            [
                pltpu.make_async_copy(
                    array.at[at], held.at[index, at], state_sems.at[index, piece]
                )
                for index, array in enumerate(state)
            ]
        )
        for piece, at in enumerate(places)
    ]
    for at, piece in zip(places, arriving):
        for copy in piece:
            copy.wait()
        result = adamw(held[0, at], held[1, at], held[2, at], held[3, at])
        weight[at, :] = result.astype(weight.dtype)
    for copy in copies:
        copy.wait()


def pack(me, keys, values, queries, state, chips):
    _, rows, features = queries.shape
    width, far = features // chips, chips - 1
    shape = state[0].shape
    pieces = math.gcd(shape[0] // 16, 4) if shape[0] % 16 == 0 else 1
    *pairs, here, weight = pl.pallas_call(
        functools.partial(pack_kernel, far),
        out_shape=[like((2, rows, width), queries)] * far
        + [like((rows, width), queries), jax.ShapeDtypeStruct(shape, jnp.bfloat16)],
        in_specs=[SMEM] + [HBM] * 7,
        out_specs=[VMEM] * (far + 2),
        scratch_shapes=[
            pltpu.VMEM((4, *shape), state[0].dtype),
            pltpu.SemaphoreType.DMA((2 * far + 1,)),
            pltpu.SemaphoreType.DMA((4, pieces)),
        ],
        compiler_params=PARAMS,
        cost_estimate=cost(8 * rows * features + 18 * state[0].size),
        name="pack",
    )(me, *map(in_hbm, (keys, values, queries, *state)))
    return pairs, here, weight


def pack_queries_kernel(me_ref, queries, *refs):
    parts, sems = refs[:-1], refs[-1]
    width = parts[0].shape[1]
    copies = [
        pltpu.make_async_copy(
            queries.at[0, :, chip_columns(me_ref, distance, width)], part, sems.at[distance - 1]
        )
        for distance, part in enumerate(parts, 1)
    ]
    for copy in copies:
        copy.start()
    for copy in copies:
        copy.wait()


def pack_queries(me, queries, chips):
    _, rows, features = queries.shape
    width, many = features // chips, chips - 1
    return pl.pallas_call(
        pack_queries_kernel,
        out_shape=[like((rows, width), queries)] * many,
        in_specs=[SMEM, HBM],
        out_specs=[VMEM] * many,
        scratch_shapes=[pltpu.SemaphoreType.DMA((many,))],
        compiler_params=PARAMS,
        cost_estimate=cost(4 * rows * features),
        name="pack_queries",
    )(me, in_hbm(queries))


def merge_kernel(index_ref, *refs):
    pieces, whole = refs[:-1], refs[-1]
    for distance, piece in enumerate(pieces):
        whole[index_ref[0] ^ distance] = piece[...]


def merge(index, pieces):
    return pl.pallas_call(
        merge_kernel,
        out_shape=like((len(pieces), *pieces[0].shape), pieces[0]),
        in_specs=[SMEM] + [VMEM] * len(pieces),
        out_specs=VMEM,
        compiler_params=PARAMS,
        cost_estimate=cost(4 * len(pieces) * pieces[0].size),
        name="merge",
    )(index, *pieces)


def places(chips, rows, pieces, width):
    tokens = [slice(index * rows, (index + 1) * rows) for index in range(2 * chips)]
    down, out_features = pieces.shape
    first, across = 2 * chips * rows, out_features // width
    weights = [
        slice(first + index * down, first + (index + 1) * down) for index in range(3 * across)
    ]
    return tokens, [weights[index * across : (index + 1) * across] for index in range(3)]


def stack_kernel(chips, *refs):
    pairs, pieces, stacked = refs[:chips], refs[chips:-1], refs[-1]
    rows, width = pairs[0].shape[1:]
    tokens, weights = places(chips, rows, pieces[0], width)
    for distance, pair in enumerate(pairs):
        stacked[tokens[2 * distance], :] = pair[0]
        stacked[tokens[2 * distance + 1], :] = pair[1]
    for piece, blocks in zip(pieces, weights):
        for index, block in enumerate(blocks):
            stacked[block, :] = piece[:, index * width : (index + 1) * width]


def stack(pairs, pieces):
    chips = len(pairs)
    _, rows, width = pairs[0].shape
    total = 2 * chips * rows + len(pieces) * pieces[0].size // width
    return pl.pallas_call(
        functools.partial(stack_kernel, chips),
        out_shape=like((total, width), pairs[0]),
        in_specs=[VMEM] * (chips + len(pieces)),
        out_specs=VMEM,
        compiler_params=PARAMS,
        cost_estimate=cost(4 * total * width),
        name="stack",
    )(*pairs, *pieces)


def collect_kernel(chips, rows, index_ref, own, last, other, weights):
    down, out_features = last.shape
    width = own.shape[1]
    _, blocks = places(chips, rows, last, width)
    for which, stacked in enumerate((own, other)):
        for distance in range(3):
            at = pl.ds(pl.multiple_of((index_ref[0] ^ distance) * down, down), down)
            for index, block in enumerate(blocks[distance]):
                weights[which, at, index * width : (index + 1) * width] = stacked[block, :]
    at = pl.ds(pl.multiple_of((index_ref[0] ^ 3) * down, down), down)
    weights[0, at, :] = last[...]
    weights[1, at, :] = jnp.zeros_like(last)


def collect(index, chips, rows, own, last, other):
    down, out_features = last.shape
    shape = (2, 4 * down, out_features)
    return pl.pallas_call(
        functools.partial(collect_kernel, chips, rows),
        out_shape=like(shape, own),
        in_specs=[SMEM] + [VMEM] * 3,
        out_specs=VMEM,
        compiler_params=PARAMS,
        cost_estimate=cost(4 * math.prod(shape)),
        name="collect",
    )(index, own, last, other)


def attend_kernel(distances, chips, me_ref, *refs):
    many = len(distances)
    parts, (own, other, attended, queries, result) = refs[:many], refs[many:]
    total, width = queries.shape
    rows = total // many
    half = width // 2
    chip, core = me_ref[0] // 2, me_ref[0] % 2
    scale = HEAD_DIM ** (-0.5) * math.log2(math.e)

    def attend_from(here):
        order = sorted(here ^ distance for distance in distances)
        place = {chip: index * rows for index, chip in enumerate(order)}
        for distance, part in zip(distances, parts):
            at = place[here ^ distance]
            queries[at : at + rows, :] = part[...]
        row = lax.broadcasted_iota(jnp.int32, (rows, 2 * rows), 0)
        column = lax.broadcasted_iota(jnp.int32, (rows, 2 * rows), 1)
        causal = jnp.where(column < rows, row, 2 * rows * core - 1) >= column

        def both(index, columns):
            at = slice(index * rows, (index + 1) * rows)
            return jnp.concatenate([own[at, columns], other[at, columns]], axis=0)

        ones = jnp.ones((2 * rows, LANES), own.dtype)
        for head in range(width // HEAD_DIM):
            columns = slice(head * HEAD_DIM, (head + 1) * HEAD_DIM)
            tiles = []
            for c in range(order[-1] + 1):
                first = min(place[chip] for chip in order if chip >= c)
                score = lax.dot_general(
                    queries[first : many * rows, columns],
                    both(2 * (here ^ c), columns),
                    (((1,), (1,)), ((), ())),
                    preferred_element_type=jnp.float32,
                )
                if c in place:
                    masked = jnp.where(causal, score[:rows], -jnp.inf)
                    later = [score[rows:]] if first + rows < many * rows else []
                    score = jnp.concatenate([masked, *later], axis=0)
                tiles.append((c, first, score))
            highest = []
            for chip in order:
                best = None
                for c, first, score in tiles:
                    if c <= chip:
                        at = place[chip] - first
                        block = score[at : at + rows]
                        best = block if best is None else jnp.maximum(best, block)
                highest.append(jnp.max(best, axis=1, keepdims=True))
            highest = jnp.concatenate(highest, axis=0)
            totals, start = None, 0
            for c, first, score in tiles:
                expons = jnp.exp2((score - highest[first:]) * scale).astype(jnp.bfloat16)
                seen = jnp.concatenate([both(2 * (here ^ c) + 1, columns), ones], axis=1)
                total = jnp.dot(expons, seen, preferred_element_type=jnp.float32)
                totals = total if totals is None else totals[first - start :] + total
                start = first
                if c in place:
                    result[first : first + rows, columns] = (
                        totals[:rows, :HEAD_DIM] / totals[:rows, HEAD_DIM:]
                    ).astype(result.dtype)
        for index, distance in enumerate(distances):
            at = place[here ^ distance]
            for part in range(2):
                attended[part, index * rows : (index + 1) * rows, :] = result[
                    at : at + rows, part * half : (part + 1) * half
                ]

    for here in range(chips):
        pl.when(chip == here)(functools.partial(attend_from, here))


def attend(me, distances, parts, own, other, chips):
    rows, width = parts[0].shape[-2:]
    length = 2 * chips * rows
    total = len(parts) * rows
    return pl.pallas_call(
        functools.partial(attend_kernel, distances, chips),
        out_shape=like((2, total, width // 2), own),
        in_specs=[SMEM] + [VMEM] * (len(parts) + 2),
        out_specs=VMEM,
        scratch_shapes=[pltpu.VMEM((total, width), own.dtype)] * 2,
        compiler_params=PARAMS,
        cost_estimate=cost(
            4 * length * width + 4 * total * width,
            4 * total * length * width,
            total * length * (width // HEAD_DIM),
        ),
        name="attend",
    )(me, *parts, own, other)


def project_kernel(chips, me_ref, index_ref, attended, weights, last, *refs):
    outs, other = refs[:-1], refs[-1]
    down = last.shape[0]
    core = me_ref[0] % 2
    other[...] = weights[1]
    other[pl.ds(pl.multiple_of((index_ref[0] ^ 3) * down, down), down), :] = last[...]
    product = jnp.dot(attended[core], weights[0], preferred_element_type=jnp.float32)
    product += jnp.dot(attended[1 - core], other[...], preferred_element_type=jnp.float32)
    rows = outs[0].shape[0]

    def give(out, distance):
        out[...] = product[distance * rows : (distance + 1) * rows].astype(out.dtype)

    if len(outs) == 1:
        give(outs[0], 0)
        return
    for out, distance in zip(outs[2:], (0, *straight(chips))):
        give(out, distance)
    for which in range(2):

        @pl.when(core == which)
        def _(which=which):
            give(outs[0], early(chips, which))
            give(outs[1], late(chips, which))


def via(core):
    return 1 + core


def late(chips, core):
    return chips - 1 ^ via(core)


def early(chips, core):
    return late(chips, 1 - core)


def straight(chips):
    return [d for d in range(1, chips - 1) if d not in (late(chips, 0), late(chips, 1))]


def project(me, index, attended, weights, last, chips, kinds):
    _, total, features = attended.shape
    width = weights.shape[2]
    return pl.pallas_call(
        functools.partial(project_kernel, chips),
        out_shape=[jax.ShapeDtypeStruct((total // len(kinds), width), kind) for kind in kinds],
        in_specs=[SMEM] * 2 + [VMEM] * 3,
        out_specs=[VMEM] * len(kinds),
        scratch_shapes=[pltpu.VMEM(weights.shape[1:], weights.dtype)],
        compiler_params=PARAMS,
        cost_estimate=cost(
            4 * total * features + 6 * features * width + 4 * total * width,
            4 * total * features * width,
        ),
        name="project",
    )(me, index, attended, weights, last)


def add_kernel(product, passed, out):
    out[...] = (product[...] + passed[...].astype(jnp.float32)).astype(out.dtype)


def add(product, passed):
    return pl.pallas_call(
        add_kernel,
        out_shape=like(passed.shape, passed),
        in_specs=[VMEM] * 2,
        out_specs=VMEM,
        compiler_params=PARAMS,
        cost_estimate=cost(8 * product.size),
        name="add",
    )(product, passed)


def make_body(seq_count, dp_count):
    chips = seq_count // 2
    far = chips - 1

    def by_core(part, distance):
        return lax.ppermute(
            part, "seq", [(i, i ^ 2 * distance(i % 2)) for i in range(seq_count)]
        )

    def to_chip(part, distance):
        return swap(part, "seq", seq_count, 2 * distance)

    def exchange(parts):
        got = [to_chip(part, d) if d else part for d, part in enumerate(parts)]
        return [*got[:-1], lax.optimization_barrier(got[-1])]

    def body(queries, keys, values, master, moment, second, gradient):
        rows = queries.shape[1]
        out_features = master.shape[1]
        me = lax.axis_index("seq").astype(jnp.int32).reshape(1)
        place = lax.axis_index("dp").astype(jnp.int32)

        farthest = pack_far(me, keys, values, chips)
        near_keys, farthest = lax.optimization_barrier((keys, farthest))
        state = (master, moment, second, gradient)
        sent_pairs, own_queries, weight = pack(me, near_keys, values, queries, state, chips)
        sent_pairs.append(farthest)
        pairs = exchange(sent_pairs)

        weight = weight[None]
        span = 1
        while 4 * span < dp_count:
            many = 4 if dp_count // span % 16 == 0 else 2
            pieces = [weight] + [swap(weight, "dp", dp_count, span * d) for d in range(1, many)]
            weight = merge((place // span % many).reshape(1), pieces)
            weight = weight.reshape(-1, *weight.shape[2:])
            span *= many
        weight = weight.reshape(-1, out_features)
        pieces = [weight] + [swap(weight, "dp", dp_count, span * d) for d in (1, 2)]
        queries, _ = lax.optimization_barrier((queries, weight))
        sent_queries = pack_queries(me, queries, chips)
        pairs, sent_queries = lax.optimization_barrier((pairs, sent_queries))
        own = stack(pairs, pieces)
        forwarded = swap(pieces[2], "dp", dp_count, span)

        other = swap(own, "seq", seq_count, 1)
        sent_queries, _ = lax.optimization_barrier((sent_queries, own))
        own_queries = exchange([own_queries, *sent_queries])

        attended = attend(me, (far,), own_queries[far:], own, other, chips)
        attended, forwarded = lax.optimization_barrier((attended, forwarded))
        near_queries, others = lax.optimization_barrier(
            (own_queries[:far], swap(forwarded, "seq", seq_count, 1))
        )
        index = (place // span % 4).reshape(1)
        weights = collect(index, chips, rows, own, forwarded, other)
        (product,) = project(me, index, attended, weights, others, chips, [attended.dtype])
        passed = by_core(product, via)
        attended = attend(me, tuple(range(far)), near_queries, own, other, chips)
        kinds = [attended.dtype, jnp.float32, jnp.float32] + [attended.dtype] * (chips - 4)
        sent, waiting, projected, *rest = project(
            me, index, attended, weights, others, chips, kinds
        )
        got = [by_core(sent, functools.partial(early, chips))]
        got += [to_chip(product, d) for d, product in zip(straight(chips), rest)]
        for product in got:
            projected += product.astype(jnp.float32)
        projected = lax.optimization_barrier(projected)
        last = by_core(add(waiting, passed), functools.partial(late, chips))
        projected += last.astype(jnp.float32)
        projected = projected.astype(jnp.bfloat16)[None]
        return (projected, adamw(master, moment, second, gradient))

    return body


def solution(mesh):
    tokens = P("dp", "seq", None)
    rows = P(("seq", "dp"), None)
    return jax.shard_map(
        make_body(mesh.shape["seq"], mesh.shape["dp"]),
        mesh=mesh,
        in_specs=(tokens,) * 3 + (rows,) * 4,
        out_specs=(tokens, rows),
        check_vma=False,
    )
```

```python
import functools
import math

import jax
import jax.numpy as jnp
from jax import lax
from jax.experimental import pallas as pl
from jax.experimental.pallas import tpu as pltpu
from jax.sharding import PartitionSpec as P

HEAD_DIM = 128
LANES = 128


beta_first = 0.9
beta_second = 0.999
learning_rate = 0.1
weight_decay = 0.1
epsilon = 1e-08
step_count = 10.0


def adamw(master, moment, second, gradient):
    moment_new = beta_first * moment + (1.0 - beta_first) * gradient
    second_new = beta_second * second + (1.0 - beta_second) * gradient * gradient
    moment_hat = moment_new / (1.0 - beta_first**step_count)
    second_hat = second_new / (1.0 - beta_second**step_count)
    return master - learning_rate * (
        moment_hat / (jnp.sqrt(second_hat) + epsilon) + weight_decay * master
    )


def swap(array, axis, count, distance):
    return lax.ppermute(array, axis, [(i, i ^ distance) for i in range(count)])


SMEM = pl.BlockSpec(memory_space=pltpu.SMEM)
VMEM = pl.BlockSpec(memory_space=pltpu.VMEM)
HBM = pl.BlockSpec(memory_space=pltpu.HBM)
PARAMS = pltpu.CompilerParams(vmem_limit_bytes=14 * 1024 * 1024)


def in_hbm(array):
    return pltpu.with_memory_space_constraint(array, pltpu.HBM)


def like(shape, array):
    return jax.ShapeDtypeStruct(shape, array.dtype)


def cost(moved, flops=0, transcendentals=0):
    return pl.CostEstimate(
        flops=flops, bytes_accessed=moved, transcendentals=transcendentals
    )


def chip_columns(me_ref, distance, width):
    return pl.ds(pl.multiple_of(((me_ref[0] // 2) ^ distance) * width, width), width)


def start_copies(copies):
    for copy in copies:
        copy.start()
    return copies


def pair_copies(me_ref, distances, keys, values, pairs, sems):
    width = pairs[0].shape[2]
    return [
        pltpu.make_async_copy(
            array.at[0, :, chip_columns(me_ref, distance, width)],
            pair.at[which],
            sems.at[2 * index + which],
        )
        for index, (distance, pair) in enumerate(zip(distances, pairs))
        for which, array in enumerate((keys, values))
    ]


def pack_far_kernel(far, me_ref, keys, values, pair, sems):
    for copy in start_copies(pair_copies(me_ref, (far,), keys, values, (pair,), sems)):
        copy.wait()


def pack_far(me, keys, values, chips):
    _, rows, features = keys.shape
    width = features // chips
    return pl.pallas_call(
        functools.partial(pack_far_kernel, chips - 1),
        out_shape=like((2, rows, width), keys),
        in_specs=[SMEM] + [HBM] * 2,
        out_specs=VMEM,
        scratch_shapes=[pltpu.SemaphoreType.DMA((2,))],
        compiler_params=PARAMS,
        cost_estimate=cost(8 * rows * width),
        name="pack_far",
    )(me, in_hbm(keys), in_hbm(values))


def pack_kernel(far, me_ref, keys, values, queries, *refs):
    state, refs = refs[:4], refs[4:]
    pairs, (here, weight, held, sems, state_sems) = refs[:far], refs[far:]
    copies = start_copies(
        pair_copies(me_ref, range(far), keys, values, pairs, sems)
        + [
            pltpu.make_async_copy(
                queries.at[0, :, chip_columns(me_ref, 0, here.shape[1])], here, sems.at[2 * far]
            )
        ]
    )
    pieces = state_sems.shape[1]
    rows = weight.shape[0] // pieces
    places = [pl.ds(piece * rows, rows) for piece in range(pieces)]
    arriving = [
        start_copies(
            [
                pltpu.make_async_copy(
                    array.at[at], held.at[index, at], state_sems.at[index, piece]
                )
                for index, array in enumerate(state)
            ]
        )
        for piece, at in enumerate(places)
    ]
    for at, piece in zip(places, arriving):
        for copy in piece:
            copy.wait()
        result = adamw(held[0, at], held[1, at], held[2, at], held[3, at])
        weight[at, :] = result.astype(weight.dtype)
    for copy in copies:
        copy.wait()


def pack(me, keys, values, queries, state, chips):
    _, rows, features = queries.shape
    width, far = features // chips, chips - 1
    shape = state[0].shape
    pieces = math.gcd(shape[0] // 16, 4) if shape[0] % 16 == 0 else 1
    *pairs, here, weight = pl.pallas_call(
        functools.partial(pack_kernel, far),
        out_shape=[like((2, rows, width), queries)] * far
        + [like((rows, width), queries), jax.ShapeDtypeStruct(shape, jnp.bfloat16)],
        in_specs=[SMEM] + [HBM] * 7,
        out_specs=[VMEM] * (far + 2),
        scratch_shapes=[
            pltpu.VMEM((4, *shape), state[0].dtype),
            pltpu.SemaphoreType.DMA((2 * far + 1,)),
            pltpu.SemaphoreType.DMA((4, pieces)),
        ],
        compiler_params=PARAMS,
        cost_estimate=cost(8 * rows * features + 18 * state[0].size),
        name="pack",
    )(me, *map(in_hbm, (keys, values, queries, *state)))
    return pairs, here, weight


def pack_queries_kernel(me_ref, queries, *refs):
    parts, sems = refs[:-1], refs[-1]
    width = parts[0].shape[1]
    copies = [
        pltpu.make_async_copy(
            queries.at[0, :, chip_columns(me_ref, distance, width)], part, sems.at[distance - 1]
        )
        for distance, part in enumerate(parts, 1)
    ]
    for copy in copies:
        copy.start()
    for copy in copies:
        copy.wait()


def pack_queries(me, queries, chips):
    _, rows, features = queries.shape
    width, many = features // chips, chips - 1
    return pl.pallas_call(
        pack_queries_kernel,
        out_shape=[like((rows, width), queries)] * many,
        in_specs=[SMEM, HBM],
        out_specs=[VMEM] * many,
        scratch_shapes=[pltpu.SemaphoreType.DMA((many,))],
        compiler_params=PARAMS,
        cost_estimate=cost(4 * rows * features),
        name="pack_queries",
    )(me, in_hbm(queries))


def merge_kernel(index_ref, *refs):
    pieces, whole = refs[:-1], refs[-1]
    for distance, piece in enumerate(pieces):
        whole[index_ref[0] ^ distance] = piece[...]


def merge(index, pieces):
    return pl.pallas_call(
        merge_kernel,
        out_shape=like((len(pieces), *pieces[0].shape), pieces[0]),
        in_specs=[SMEM] + [VMEM] * len(pieces),
        out_specs=VMEM,
        compiler_params=PARAMS,
        cost_estimate=cost(4 * len(pieces) * pieces[0].size),
        name="merge",
    )(index, *pieces)


def places(chips, rows, pieces, width):
    tokens = [slice(index * rows, (index + 1) * rows) for index in range(2 * chips)]
    down, out_features = pieces.shape
    first, across = 2 * chips * rows, out_features // width
    weights = [
        slice(first + index * down, first + (index + 1) * down) for index in range(3 * across)
    ]
    return tokens, [weights[index * across : (index + 1) * across] for index in range(3)]


def stack_kernel(chips, *refs):
    pairs, pieces, stacked = refs[:chips], refs[chips:-1], refs[-1]
    rows, width = pairs[0].shape[1:]
    tokens, weights = places(chips, rows, pieces[0], width)
    for distance, pair in enumerate(pairs):
        stacked[tokens[2 * distance], :] = pair[0]
        stacked[tokens[2 * distance + 1], :] = pair[1]
    for piece, blocks in zip(pieces, weights):
        for index, block in enumerate(blocks):
            stacked[block, :] = piece[:, index * width : (index + 1) * width]


def stack(pairs, pieces):
    chips = len(pairs)
    _, rows, width = pairs[0].shape
    total = 2 * chips * rows + len(pieces) * pieces[0].size // width
    return pl.pallas_call(
        functools.partial(stack_kernel, chips),
        out_shape=like((total, width), pairs[0]),
        in_specs=[VMEM] * (chips + len(pieces)),
        out_specs=VMEM,
        compiler_params=PARAMS,
        cost_estimate=cost(4 * total * width),
        name="stack",
    )(*pairs, *pieces)


def collect_kernel(chips, rows, index_ref, own, last, other, weights):
    down, out_features = last.shape
    width = own.shape[1]
    _, blocks = places(chips, rows, last, width)
    for which, stacked in enumerate((own, other)):
        for distance in range(3):
            at = pl.ds(pl.multiple_of((index_ref[0] ^ distance) * down, down), down)
            for index, block in enumerate(blocks[distance]):
                weights[which, at, index * width : (index + 1) * width] = stacked[block, :]
    at = pl.ds(pl.multiple_of((index_ref[0] ^ 3) * down, down), down)
    weights[0, at, :] = last[...]
    weights[1, at, :] = jnp.zeros_like(last)


def collect(index, chips, rows, own, last, other):
    down, out_features = last.shape
    shape = (2, 4 * down, out_features)
    return pl.pallas_call(
        functools.partial(collect_kernel, chips, rows),
        out_shape=like(shape, own),
        in_specs=[SMEM] + [VMEM] * 3,
        out_specs=VMEM,
        compiler_params=PARAMS,
        cost_estimate=cost(4 * math.prod(shape)),
        name="collect",
    )(index, own, last, other)


def attend_kernel(distances, chips, me_ref, *refs):
    many = len(distances)
    parts, (own, other, attended, queries, result) = refs[:many], refs[many:]
    total, width = queries.shape
    rows = total // many
    half = width // 2
    chip, core = me_ref[0] // 2, me_ref[0] % 2
    scale = HEAD_DIM ** (-0.5) * math.log2(math.e)

    def attend_from(here):
        order = sorted(here ^ distance for distance in distances)
        place = {chip: index * rows for index, chip in enumerate(order)}
        for distance, part in zip(distances, parts):
            at = place[here ^ distance]
            queries[at : at + rows, :] = part[...]
        row = lax.broadcasted_iota(jnp.int32, (rows, 2 * rows), 0)
        column = lax.broadcasted_iota(jnp.int32, (rows, 2 * rows), 1)
        causal = jnp.where(column < rows, row, 2 * rows * core - 1) >= column

        def both(index, columns):
            at = slice(index * rows, (index + 1) * rows)
            return jnp.concatenate([own[at, columns], other[at, columns]], axis=0)

        ones = jnp.ones((2 * rows, LANES), own.dtype)
        def score_tiles(columns):
            tiles = []
            for c in range(order[-1] + 1):
                first = min(place[chip] for chip in order if chip >= c)
                score = lax.dot_general(
                    queries[first : many * rows, columns],
                    both(2 * (here ^ c), columns),
                    (((1,), (1,)), ((), ())),
                    preferred_element_type=jnp.float32,
                )
                if c in place:
                    masked = jnp.where(causal, score[:rows], -jnp.inf)
                    later = [score[rows:]] if first + rows < many * rows else []
                    score = jnp.concatenate([masked, *later], axis=0)
                tiles.append((c, first, score))
            return tiles

        def exponentials(tiles):
            highest = []
            for chip in order:
                best = None
                for c, first, score in tiles:
                    if c <= chip:
                        at = place[chip] - first
                        block = score[at : at + rows]
                        best = block if best is None else jnp.maximum(best, block)
                highest.append(jnp.max(best, axis=1, keepdims=True))
            highest = jnp.concatenate(highest, axis=0)
            return [
                (c, first, jnp.exp2((score - highest[first:]) * scale).astype(jnp.bfloat16))
                for c, first, score in tiles
            ]

        def combine(columns, tiles):
            totals, start = None, 0
            for c, first, expons in tiles:
                seen = jnp.concatenate([both(2 * (here ^ c) + 1, columns), ones], axis=1)
                total = jnp.dot(expons, seen, preferred_element_type=jnp.float32)
                totals = total if totals is None else totals[first - start :] + total
                start = first
                if c in place:
                    result[first : first + rows, columns] = (
                        totals[:rows, :HEAD_DIM] / totals[:rows, HEAD_DIM:]
                    ).astype(result.dtype)

        heads = [
            slice(head * HEAD_DIM, (head + 1) * HEAD_DIM) for head in range(width // HEAD_DIM)
        ]
        scores = [score_tiles(columns) for columns in heads]
        for columns, tiles in zip(heads, scores):
            combine(columns, exponentials(tiles))
        for index, distance in enumerate(distances):
            at = place[here ^ distance]
            for part in range(2):
                attended[part, index * rows : (index + 1) * rows, :] = result[
                    at : at + rows, part * half : (part + 1) * half
                ]

    for here in range(chips):
        pl.when(chip == here)(functools.partial(attend_from, here))


def attend(me, distances, parts, own, other, chips):
    rows, width = parts[0].shape[-2:]
    length = 2 * chips * rows
    total = len(parts) * rows
    return pl.pallas_call(
        functools.partial(attend_kernel, distances, chips),
        out_shape=like((2, total, width // 2), own),
        in_specs=[SMEM] + [VMEM] * (len(parts) + 2),
        out_specs=VMEM,
        scratch_shapes=[pltpu.VMEM((total, width), own.dtype)] * 2,
        compiler_params=PARAMS,
        cost_estimate=cost(
            4 * length * width + 4 * total * width,
            4 * total * length * width,
            total * length * (width // HEAD_DIM),
        ),
        name="attend",
    )(me, *parts, own, other)


def project_kernel(chips, me_ref, index_ref, attended, weights, last, *refs):
    outs, other = refs[:-1], refs[-1]
    down = last.shape[0]
    core = me_ref[0] % 2
    other[...] = weights[1]
    other[pl.ds(pl.multiple_of((index_ref[0] ^ 3) * down, down), down), :] = last[...]
    product = jnp.dot(attended[core], weights[0], preferred_element_type=jnp.float32)
    product += jnp.dot(attended[1 - core], other[...], preferred_element_type=jnp.float32)
    rows = outs[0].shape[0]

    def give(out, distance):
        out[...] = product[distance * rows : (distance + 1) * rows].astype(out.dtype)

    if len(outs) == 1:
        give(outs[0], 0)
        return
    for out, distance in zip(outs[2:], (0, *straight(chips))):
        give(out, distance)
    for which in range(2):

        @pl.when(core == which)
        def _(which=which):
            give(outs[0], early(chips, which))
            give(outs[1], late(chips, which))


def via(core):
    return 1 + core


def late(chips, core):
    return chips - 1 ^ via(core)


def early(chips, core):
    return late(chips, 1 - core)


def straight(chips):
    return [d for d in range(1, chips - 1) if d not in (late(chips, 0), late(chips, 1))]


def project(me, index, attended, weights, last, chips, kinds):
    _, total, features = attended.shape
    width = weights.shape[2]
    return pl.pallas_call(
        functools.partial(project_kernel, chips),
        out_shape=[jax.ShapeDtypeStruct((total // len(kinds), width), kind) for kind in kinds],
        in_specs=[SMEM] * 2 + [VMEM] * 3,
        out_specs=[VMEM] * len(kinds),
        scratch_shapes=[pltpu.VMEM(weights.shape[1:], weights.dtype)],
        compiler_params=PARAMS,
        cost_estimate=cost(
            4 * total * features + 6 * features * width + 4 * total * width,
            4 * total * features * width,
        ),
        name="project",
    )(me, index, attended, weights, last)


def add_kernel(product, passed, out):
    out[...] = (product[...] + passed[...].astype(jnp.float32)).astype(out.dtype)


def add(product, passed):
    return pl.pallas_call(
        add_kernel,
        out_shape=like(passed.shape, passed),
        in_specs=[VMEM] * 2,
        out_specs=VMEM,
        compiler_params=PARAMS,
        cost_estimate=cost(8 * product.size),
        name="add",
    )(product, passed)


def make_body(seq_count, dp_count):
    chips = seq_count // 2
    far = chips - 1

    def by_core(part, distance):
        return lax.ppermute(
            part, "seq", [(i, i ^ 2 * distance(i % 2)) for i in range(seq_count)]
        )

    def to_chip(part, distance):
        return swap(part, "seq", seq_count, 2 * distance)

    def exchange(parts):
        got = [to_chip(part, d) if d else part for d, part in enumerate(parts)]
        return [*got[:-1], lax.optimization_barrier(got[-1])]

    def body(queries, keys, values, master, moment, second, gradient):
        rows = queries.shape[1]
        out_features = master.shape[1]
        me = lax.axis_index("seq").astype(jnp.int32).reshape(1)
        place = lax.axis_index("dp").astype(jnp.int32)

        farthest = pack_far(me, keys, values, chips)
        near_keys, farthest = lax.optimization_barrier((keys, farthest))
        state = (master, moment, second, gradient)
        sent_pairs, own_queries, weight = pack(me, near_keys, values, queries, state, chips)
        sent_pairs.append(farthest)
        pairs = exchange(sent_pairs)

        weight = weight[None]
        span = 1
        while 4 * span < dp_count:
            many = 4 if dp_count // span % 16 == 0 else 2
            pieces = [weight] + [swap(weight, "dp", dp_count, span * d) for d in range(1, many)]
            weight = merge((place // span % many).reshape(1), pieces)
            weight = weight.reshape(-1, *weight.shape[2:])
            span *= many
        weight = weight.reshape(-1, out_features)
        pieces = [weight] + [swap(weight, "dp", dp_count, span * d) for d in (1, 2)]
        queries, _ = lax.optimization_barrier((queries, weight))
        sent_queries = pack_queries(me, queries, chips)
        pairs, sent_queries = lax.optimization_barrier((pairs, sent_queries))
        own = stack(pairs, pieces)
        forwarded = swap(pieces[2], "dp", dp_count, span)

        other = swap(own, "seq", seq_count, 1)
        sent_queries, _ = lax.optimization_barrier((sent_queries, own))
        own_queries = exchange([own_queries, *sent_queries])

        attended = attend(me, (far,), own_queries[far:], own, other, chips)
        attended, forwarded = lax.optimization_barrier((attended, forwarded))
        near_queries, others = lax.optimization_barrier(
            (own_queries[:far], swap(forwarded, "seq", seq_count, 1))
        )
        index = (place // span % 4).reshape(1)
        weights = collect(index, chips, rows, own, forwarded, other)
        (product,) = project(me, index, attended, weights, others, chips, [attended.dtype])
        passed = by_core(product, via)
        attended = attend(me, tuple(range(far)), near_queries, own, other, chips)
        kinds = [attended.dtype, jnp.float32, jnp.float32] + [attended.dtype] * (chips - 4)
        sent, waiting, projected, *rest = project(
            me, index, attended, weights, others, chips, kinds
        )
        got = [by_core(sent, functools.partial(early, chips))]
        got += [to_chip(product, d) for d, product in zip(straight(chips), rest)]
        for product in got:
            projected += product.astype(jnp.float32)
        projected = lax.optimization_barrier(projected)
        last = by_core(add(waiting, passed), functools.partial(late, chips))
        projected += last.astype(jnp.float32)
        projected = projected.astype(jnp.bfloat16)[None]
        return (projected, adamw(master, moment, second, gradient))

    return body


def solution(mesh):
    tokens = P("dp", "seq", None)
    rows = P(("seq", "dp"), None)
    return jax.shard_map(
        make_body(mesh.shape["seq"], mesh.shape["dp"]),
        mesh=mesh,
        in_specs=(tokens,) * 3 + (rows,) * 4,
        out_specs=(tokens, rows),
        check_vma=False,
    )
```

```python
import functools
import math

import jax
import jax.numpy as jnp
from jax import lax
from jax.experimental import pallas as pl
from jax.experimental.pallas import tpu as pltpu
from jax.sharding import PartitionSpec as P

HEAD_DIM = 128
LANES = 128


beta_first = 0.9
beta_second = 0.999
learning_rate = 0.1
weight_decay = 0.1
epsilon = 1e-08
step_count = 10.0


def adamw(master, moment, second, gradient):
    moment_new = beta_first * moment + (1.0 - beta_first) * gradient
    second_new = beta_second * second + (1.0 - beta_second) * gradient * gradient
    moment_hat = moment_new / (1.0 - beta_first**step_count)
    second_hat = second_new / (1.0 - beta_second**step_count)
    return master - learning_rate * (
        moment_hat / (jnp.sqrt(second_hat) + epsilon) + weight_decay * master
    )


def swap(array, axis, count, distance):
    return lax.ppermute(array, axis, [(i, i ^ distance) for i in range(count)])


SMEM = pl.BlockSpec(memory_space=pltpu.SMEM)
VMEM = pl.BlockSpec(memory_space=pltpu.VMEM)
HBM = pl.BlockSpec(memory_space=pltpu.HBM)
PARAMS = pltpu.CompilerParams(vmem_limit_bytes=14 * 1024 * 1024)


def in_hbm(array):
    return pltpu.with_memory_space_constraint(array, pltpu.HBM)


def like(shape, array):
    return jax.ShapeDtypeStruct(shape, array.dtype)


def cost(moved, flops=0, transcendentals=0):
    return pl.CostEstimate(
        flops=flops, bytes_accessed=moved, transcendentals=transcendentals
    )


def chip_columns(me_ref, distance, width):
    return pl.ds(pl.multiple_of(((me_ref[0] // 2) ^ distance) * width, width), width)


def start_copies(copies):
    for copy in copies:
        copy.start()
    return copies


def pair_copies(me_ref, distances, keys, values, pairs, sems):
    width = pairs[0].shape[2]
    return [
        pltpu.make_async_copy(
            array.at[0, :, chip_columns(me_ref, distance, width)],
            pair.at[which],
            sems.at[2 * index + which],
        )
        for index, (distance, pair) in enumerate(zip(distances, pairs))
        for which, array in enumerate((keys, values))
    ]


def pack_far_kernel(far, me_ref, keys, values, pair, sems):
    for copy in start_copies(pair_copies(me_ref, (far,), keys, values, (pair,), sems)):
        copy.wait()


def pack_far(me, keys, values, chips):
    _, rows, features = keys.shape
    width = features // chips
    return pl.pallas_call(
        functools.partial(pack_far_kernel, chips - 1),
        out_shape=like((2, rows, width), keys),
        in_specs=[SMEM] + [HBM] * 2,
        out_specs=VMEM,
        scratch_shapes=[pltpu.SemaphoreType.DMA((2,))],
        compiler_params=PARAMS,
        cost_estimate=cost(8 * rows * width),
        name="pack_far",
    )(me, in_hbm(keys), in_hbm(values))


def pack_kernel(far, me_ref, keys, values, queries, *refs):
    state, refs = refs[:4], refs[4:]
    pairs, (here, weight, held, sems, state_sems) = refs[:far], refs[far:]
    copies = start_copies(
        pair_copies(me_ref, range(far), keys, values, pairs, sems)
        + [
            pltpu.make_async_copy(
                queries.at[0, :, chip_columns(me_ref, 0, here.shape[1])], here, sems.at[2 * far]
            )
        ]
    )
    pieces = state_sems.shape[1]
    rows = weight.shape[0] // pieces
    places = [pl.ds(piece * rows, rows) for piece in range(pieces)]
    arriving = [
        start_copies(
            [
                pltpu.make_async_copy(
                    array.at[at], held.at[index, at], state_sems.at[index, piece]
                )
                for index, array in enumerate(state)
            ]
        )
        for piece, at in enumerate(places)
    ]
    for at, piece in zip(places, arriving):
        for copy in piece:
            copy.wait()
        result = adamw(held[0, at], held[1, at], held[2, at], held[3, at])
        weight[at, :] = result.astype(weight.dtype)
    for copy in copies:
        copy.wait()


def pack(me, keys, values, queries, state, chips):
    _, rows, features = queries.shape
    width, far = features // chips, chips - 1
    shape = state[0].shape
    pieces = math.gcd(shape[0] // 16, 4) if shape[0] % 16 == 0 else 1
    *pairs, here, weight = pl.pallas_call(
        functools.partial(pack_kernel, far),
        out_shape=[like((2, rows, width), queries)] * far
        + [like((rows, width), queries), jax.ShapeDtypeStruct(shape, jnp.bfloat16)],
        in_specs=[SMEM] + [HBM] * 7,
        out_specs=[VMEM] * (far + 2),
        scratch_shapes=[
            pltpu.VMEM((4, *shape), state[0].dtype),
            pltpu.SemaphoreType.DMA((2 * far + 1,)),
            pltpu.SemaphoreType.DMA((4, pieces)),
        ],
        compiler_params=PARAMS,
        cost_estimate=cost(8 * rows * features + 18 * state[0].size),
        name="pack",
    )(me, *map(in_hbm, (keys, values, queries, *state)))
    return pairs, here, weight


def pack_queries_kernel(me_ref, queries, *refs):
    parts, sems = refs[:-1], refs[-1]
    width = parts[0].shape[1]
    copies = [
        pltpu.make_async_copy(
            queries.at[0, :, chip_columns(me_ref, distance, width)], part, sems.at[distance - 1]
        )
        for distance, part in enumerate(parts, 1)
    ]
    for copy in copies:
        copy.start()
    for copy in copies:
        copy.wait()


def pack_queries(me, queries, chips):
    _, rows, features = queries.shape
    width, many = features // chips, chips - 1
    return pl.pallas_call(
        pack_queries_kernel,
        out_shape=[like((rows, width), queries)] * many,
        in_specs=[SMEM, HBM],
        out_specs=[VMEM] * many,
        scratch_shapes=[pltpu.SemaphoreType.DMA((many,))],
        compiler_params=PARAMS,
        cost_estimate=cost(4 * rows * features),
        name="pack_queries",
    )(me, in_hbm(queries))


def merge_kernel(index_ref, *refs):
    pieces, whole = refs[:-1], refs[-1]
    for distance, piece in enumerate(pieces):
        whole[index_ref[0] ^ distance] = piece[...]


def merge(index, pieces):
    return pl.pallas_call(
        merge_kernel,
        out_shape=like((len(pieces), *pieces[0].shape), pieces[0]),
        in_specs=[SMEM] + [VMEM] * len(pieces),
        out_specs=VMEM,
        compiler_params=PARAMS,
        cost_estimate=cost(4 * len(pieces) * pieces[0].size),
        name="merge",
    )(index, *pieces)


def hold_kernel(source, target):
    target[...] = source[...]


def hold(array):
    return pl.pallas_call(
        hold_kernel,
        out_shape=like(array.shape, array),
        in_specs=[VMEM],
        out_specs=VMEM,
        compiler_params=PARAMS,
        cost_estimate=cost(4 * array.size, 3 * 10**10),
        name="hold",
    )(array)


def places(chips, rows, pieces, width):
    tokens = [slice(index * rows, (index + 1) * rows) for index in range(2 * chips)]
    down, out_features = pieces.shape
    first, across = 2 * chips * rows, out_features // width
    weights = [
        slice(first + index * down, first + (index + 1) * down) for index in range(3 * across)
    ]
    return tokens, [weights[index * across : (index + 1) * across] for index in range(3)]


def stack_kernel(chips, *refs):
    pairs, pieces, stacked = refs[:chips], refs[chips:-1], refs[-1]
    rows, width = pairs[0].shape[1:]
    tokens, weights = places(chips, rows, pieces[0], width)
    for distance, pair in enumerate(pairs):
        stacked[tokens[2 * distance], :] = pair[0]
        stacked[tokens[2 * distance + 1], :] = pair[1]
    for piece, blocks in zip(pieces, weights):
        for index, block in enumerate(blocks):
            stacked[block, :] = piece[:, index * width : (index + 1) * width]


def stack(pairs, pieces):
    chips = len(pairs)
    _, rows, width = pairs[0].shape
    total = 2 * chips * rows + len(pieces) * pieces[0].size // width
    return pl.pallas_call(
        functools.partial(stack_kernel, chips),
        out_shape=like((total, width), pairs[0]),
        in_specs=[VMEM] * (chips + len(pieces)),
        out_specs=VMEM,
        compiler_params=PARAMS,
        cost_estimate=cost(4 * total * width),
        name="stack",
    )(*pairs, *pieces)


def collect_kernel(chips, rows, index_ref, own, last, other, weights):
    down, out_features = last.shape
    width = own.shape[1]
    _, blocks = places(chips, rows, last, width)
    for which, stacked in enumerate((own, other)):
        for distance in range(3):
            at = pl.ds(pl.multiple_of((index_ref[0] ^ distance) * down, down), down)
            for index, block in enumerate(blocks[distance]):
                weights[which, at, index * width : (index + 1) * width] = stacked[block, :]
    at = pl.ds(pl.multiple_of((index_ref[0] ^ 3) * down, down), down)
    weights[0, at, :] = last[...]
    weights[1, at, :] = jnp.zeros_like(last)


def collect(index, chips, rows, own, last, other):
    down, out_features = last.shape
    shape = (2, 4 * down, out_features)
    return pl.pallas_call(
        functools.partial(collect_kernel, chips, rows),
        out_shape=like(shape, own),
        in_specs=[SMEM] + [VMEM] * 3,
        out_specs=VMEM,
        compiler_params=PARAMS,
        cost_estimate=cost(0),
        name="collect",
    )(index, own, last, other)


def attend_kernel(distances, chips, me_ref, *refs):
    many = len(distances)
    parts, (own, other, attended, queries, result) = refs[:many], refs[many:]
    total, width = queries.shape
    rows = total // many
    half = width // 2
    chip, core = me_ref[0] // 2, me_ref[0] % 2
    scale = HEAD_DIM ** (-0.5) * math.log2(math.e)

    def attend_from(here):
        order = sorted(here ^ distance for distance in distances)
        place = {chip: index * rows for index, chip in enumerate(order)}
        for distance, part in zip(distances, parts):
            at = place[here ^ distance]
            queries[at : at + rows, :] = part[...]
        row = lax.broadcasted_iota(jnp.int32, (rows, 2 * rows), 0)
        column = lax.broadcasted_iota(jnp.int32, (rows, 2 * rows), 1)
        causal = jnp.where(column < rows, row, 2 * rows * core - 1) >= column

        def both(index, columns):
            at = slice(index * rows, (index + 1) * rows)
            return jnp.concatenate([own[at, columns], other[at, columns]], axis=0)

        ones = jnp.ones((2 * rows, LANES), own.dtype)
        def score_tiles(columns):
            tiles = []
            for c in range(order[-1] + 1):
                first = min(place[chip] for chip in order if chip >= c)
                score = lax.dot_general(
                    queries[first : many * rows, columns],
                    both(2 * (here ^ c), columns),
                    (((1,), (1,)), ((), ())),
                    preferred_element_type=jnp.float32,
                )
                if c in place:
                    masked = jnp.where(causal, score[:rows], -jnp.inf)
                    later = [score[rows:]] if first + rows < many * rows else []
                    score = jnp.concatenate([masked, *later], axis=0)
                tiles.append((c, first, score))
            return tiles

        def exponentials(tiles):
            highest = []
            for chip in order:
                best = None
                for c, first, score in tiles:
                    if c <= chip:
                        at = place[chip] - first
                        block = score[at : at + rows]
                        best = block if best is None else jnp.maximum(best, block)
                highest.append(jnp.max(best, axis=1, keepdims=True))
            highest = jnp.concatenate(highest, axis=0)
            return [
                (c, first, jnp.exp2((score - highest[first:]) * scale).astype(jnp.bfloat16))
                for c, first, score in tiles
            ]

        def combine(columns, tiles):
            totals, start = None, 0
            for c, first, expons in tiles:
                seen = jnp.concatenate([both(2 * (here ^ c) + 1, columns), ones], axis=1)
                total = jnp.dot(expons, seen, preferred_element_type=jnp.float32)
                totals = total if totals is None else totals[first - start :] + total
                start = first
                if c in place:
                    result[first : first + rows, columns] = (
                        totals[:rows, :HEAD_DIM] / totals[:rows, HEAD_DIM:]
                    ).astype(result.dtype)

        heads = [
            slice(head * HEAD_DIM, (head + 1) * HEAD_DIM) for head in range(width // HEAD_DIM)
        ]
        scores = [score_tiles(columns) for columns in heads]
        for columns, tiles in zip(heads, scores):
            combine(columns, exponentials(tiles))
        for index, distance in enumerate(distances):
            at = place[here ^ distance]
            for part in range(2):
                attended[part, index * rows : (index + 1) * rows, :] = result[
                    at : at + rows, part * half : (part + 1) * half
                ]

    for here in range(chips):
        pl.when(chip == here)(functools.partial(attend_from, here))


def attend(me, distances, parts, own, other, chips):
    rows, width = parts[0].shape[-2:]
    length = 2 * chips * rows
    total = len(parts) * rows
    return pl.pallas_call(
        functools.partial(attend_kernel, distances, chips),
        out_shape=like((2, total, width // 2), own),
        in_specs=[SMEM] + [VMEM] * (len(parts) + 2),
        out_specs=VMEM,
        scratch_shapes=[pltpu.VMEM((total, width), own.dtype)] * 2,
        compiler_params=PARAMS,
        cost_estimate=cost(0, 10**10 * (len(distances) - 1)),
        name="attend",
    )(me, *parts, own, other)


def project_kernel(chips, held, me_ref, index_ref, attended, weights, last, *refs):
    outs, other = refs[held:-1], refs[-1]
    down = last.shape[0]
    core = me_ref[0] % 2
    other[...] = weights[1]
    other[pl.ds(pl.multiple_of((index_ref[0] ^ 3) * down, down), down), :] = last[...]
    product = jnp.dot(attended[core], weights[0], preferred_element_type=jnp.float32)
    product += jnp.dot(attended[1 - core], other[...], preferred_element_type=jnp.float32)
    rows = outs[0].shape[0]

    def give(out, distance):
        out[...] = product[distance * rows : (distance + 1) * rows].astype(out.dtype)

    if len(outs) == 1:
        give(outs[0], 0)
        return
    for out, distance in zip(outs[2:], (0, *straight(chips))):
        give(out, distance)
    for which in range(2):

        @pl.when(core == which)
        def _(which=which):
            give(outs[0], early(chips, which))
            give(outs[1], late(chips, which))


def via(core):
    return 1 + core


def late(chips, core):
    return chips - 1 ^ via(core)


def early(chips, core):
    return late(chips, 1 - core)


def straight(chips):
    return [d for d in range(1, chips - 1) if d not in (late(chips, 0), late(chips, 1))]


def project(me, index, attended, weights, last, chips, kinds, held=()):
    _, total, features = attended.shape
    width = weights.shape[2]
    return pl.pallas_call(
        functools.partial(project_kernel, chips, len(held)),
        out_shape=[jax.ShapeDtypeStruct((total // len(kinds), width), kind) for kind in kinds],
        in_specs=[SMEM] * 2 + [VMEM] * (3 + len(held)),
        out_specs=[VMEM] * len(kinds),
        scratch_shapes=[pltpu.VMEM(weights.shape[1:], weights.dtype)],
        compiler_params=PARAMS,
        cost_estimate=cost(0),
        name="project",
    )(me, index, attended, weights, last, *held)


def add_kernel(product, passed, out):
    out[...] = (product[...] + passed[...].astype(jnp.float32)).astype(out.dtype)


def add(product, passed):
    return pl.pallas_call(
        add_kernel,
        out_shape=like(passed.shape, passed),
        in_specs=[VMEM] * 2,
        out_specs=VMEM,
        compiler_params=PARAMS,
        cost_estimate=cost(8 * product.size),
        name="add",
    )(product, passed)


def make_body(seq_count, dp_count):
    chips = seq_count // 2
    far = chips - 1

    def by_core(part, distance):
        return lax.ppermute(
            part, "seq", [(i, i ^ 2 * distance(i % 2)) for i in range(seq_count)]
        )

    def to_chip(part, distance):
        return swap(part, "seq", seq_count, 2 * distance)

    def exchange(parts):
        got = [to_chip(part, d) if d else part for d, part in enumerate(parts)]
        return [*got[:-1], lax.optimization_barrier(got[-1])]

    def body(queries, keys, values, master, moment, second, gradient):
        rows = queries.shape[1]
        out_features = master.shape[1]
        me = lax.axis_index("seq").astype(jnp.int32).reshape(1)
        place = lax.axis_index("dp").astype(jnp.int32)

        farthest = pack_far(me, keys, values, chips)
        near_keys, farthest = lax.optimization_barrier((keys, farthest))
        state = (master, moment, second, gradient)
        sent_pairs, own_queries, weight = pack(me, near_keys, values, queries, state, chips)
        sent_pairs.append(farthest)
        pairs = exchange(sent_pairs)

        weight = weight[None]
        span = 1
        while 4 * span < dp_count:
            many = 4 if dp_count // span % 16 == 0 else 2
            pieces = [weight] + [swap(weight, "dp", dp_count, span * d) for d in range(1, many)]
            weight = merge((place // span % many).reshape(1), pieces)
            weight = weight.reshape(-1, *weight.shape[2:])
            span *= many
        weight = weight.reshape(-1, out_features)
        pieces = [weight] + [swap(weight, "dp", dp_count, span * d) for d in (1, 2)]
        queries, _ = lax.optimization_barrier((queries, weight))
        sent_queries = pack_queries(me, queries, chips)
        pieces[2], sent_queries = lax.optimization_barrier((pieces[2], sent_queries))
        own = stack(pairs, pieces)
        forwarded = hold(swap(pieces[2], "dp", dp_count, span))

        other = swap(own, "seq", seq_count, 1)
        sent_queries, _ = lax.optimization_barrier((sent_queries, own))
        near_parts, forwarded = lax.optimization_barrier((sent_queries[:-1], forwarded))
        sent_queries = [*near_parts, sent_queries[-1]]
        own_queries = exchange([own_queries, *sent_queries])

        attended = attend(me, (far,), own_queries[far:], own, other, chips)
        near_queries, others = own_queries[:far], swap(forwarded, "seq", seq_count, 1)
        index = (place // span % 4).reshape(1)
        weights = collect(index, chips, rows, own, forwarded, other)
        (product,) = project(me, index, attended, weights, others, chips, [attended.dtype])
        passed = by_core(product, via)
        attended = attend(me, tuple(range(far)), near_queries, own, other, chips)
        kinds = [attended.dtype, jnp.float32, jnp.float32] + [attended.dtype] * (chips - 4)
        sent, waiting, projected, *rest = project(
            me, index, attended, weights, others, chips, kinds, near_queries
        )
        got = [by_core(sent, functools.partial(early, chips))]
        got += [to_chip(product, d) for d, product in zip(straight(chips), rest)]
        for product in got:
            projected += product.astype(jnp.float32)
        projected = lax.optimization_barrier(projected)
        last = by_core(add(waiting, passed), functools.partial(late, chips))
        projected += last.astype(jnp.float32)
        projected = projected.astype(jnp.bfloat16)[None]
        return (projected, adamw(master, moment, second, gradient))

    return body


def solution(mesh):
    tokens = P("dp", "seq", None)
    rows = P(("seq", "dp"), None)
    return jax.shard_map(
        make_body(mesh.shape["seq"], mesh.shape["dp"]),
        mesh=mesh,
        in_specs=(tokens,) * 3 + (rows,) * 4,
        out_specs=(tokens, rows),
        check_vma=False,
    )
```

```python
import functools
import math

import jax
import jax.numpy as jnp
from jax import lax
from jax.experimental import pallas as pl
from jax.experimental.pallas import tpu as pltpu
from jax.sharding import PartitionSpec as P

HEAD_DIM = 128
LANES = 128


beta_first = 0.9
beta_second = 0.999
learning_rate = 0.1
weight_decay = 0.1
epsilon = 1e-08
step_count = 10.0


def adamw(master, moment, second, gradient):
    moment_new = beta_first * moment + (1.0 - beta_first) * gradient
    second_new = beta_second * second + (1.0 - beta_second) * gradient * gradient
    moment_hat = moment_new / (1.0 - beta_first**step_count)
    second_hat = second_new / (1.0 - beta_second**step_count)
    return master - learning_rate * (
        moment_hat / (jnp.sqrt(second_hat) + epsilon) + weight_decay * master
    )


def swap(array, axis, count, distance):
    return lax.ppermute(array, axis, [(i, i ^ distance) for i in range(count)])


SMEM = pl.BlockSpec(memory_space=pltpu.SMEM)
VMEM = pl.BlockSpec(memory_space=pltpu.VMEM)
HBM = pl.BlockSpec(memory_space=pltpu.HBM)
PARAMS = pltpu.CompilerParams(vmem_limit_bytes=14 * 1024 * 1024)


def in_hbm(array):
    return pltpu.with_memory_space_constraint(array, pltpu.HBM)


def like(shape, array):
    return jax.ShapeDtypeStruct(shape, array.dtype)


def cost(moved, flops=0, transcendentals=0):
    return pl.CostEstimate(
        flops=flops, bytes_accessed=moved, transcendentals=transcendentals
    )


def chip_columns(me_ref, distance, width):
    return pl.ds(pl.multiple_of(((me_ref[0] // 2) ^ distance) * width, width), width)


def start_copies(copies):
    for copy in copies:
        copy.start()
    return copies


def pair_copies(me_ref, distances, keys, values, pairs, sems):
    width = pairs[0].shape[2]
    return [
        pltpu.make_async_copy(
            array.at[0, :, chip_columns(me_ref, distance, width)],
            pair.at[which],
            sems.at[2 * index + which],
        )
        for index, (distance, pair) in enumerate(zip(distances, pairs))
        for which, array in enumerate((keys, values))
    ]


def pack_far_kernel(far, me_ref, keys, values, pair, sems):
    for copy in start_copies(pair_copies(me_ref, (far,), keys, values, (pair,), sems)):
        copy.wait()


def pack_far(me, keys, values, chips):
    _, rows, features = keys.shape
    width = features // chips
    return pl.pallas_call(
        functools.partial(pack_far_kernel, chips - 1),
        out_shape=like((2, rows, width), keys),
        in_specs=[SMEM] + [HBM] * 2,
        out_specs=VMEM,
        scratch_shapes=[pltpu.SemaphoreType.DMA((2,))],
        compiler_params=PARAMS,
        cost_estimate=cost(8 * rows * width),
        name="pack_far",
    )(me, in_hbm(keys), in_hbm(values))


def pack_kernel(far, me_ref, keys, values, queries, *refs):
    state, refs = refs[:4], refs[4:]
    pairs, (here, weight, held, sems, state_sems) = refs[:far], refs[far:]
    copies = start_copies(
        pair_copies(me_ref, range(far), keys, values, pairs, sems)
        + [
            pltpu.make_async_copy(
                queries.at[0, :, chip_columns(me_ref, 0, here.shape[1])], here, sems.at[2 * far]
            )
        ]
    )
    pieces = state_sems.shape[1]
    rows = weight.shape[0] // pieces
    places = [pl.ds(piece * rows, rows) for piece in range(pieces)]
    arriving = [
        start_copies(
            [
                pltpu.make_async_copy(
                    array.at[at], held.at[index, at], state_sems.at[index, piece]
                )
                for index, array in enumerate(state)
            ]
        )
        for piece, at in enumerate(places)
    ]
    for at, piece in zip(places, arriving):
        for copy in piece:
            copy.wait()
        result = adamw(held[0, at], held[1, at], held[2, at], held[3, at])
        weight[at, :] = result.astype(weight.dtype)
    for copy in copies:
        copy.wait()


def pack(me, keys, values, queries, state, chips):
    _, rows, features = queries.shape
    width, far = features // chips, chips - 1
    shape = state[0].shape
    pieces = math.gcd(shape[0] // 16, 4) if shape[0] % 16 == 0 else 1
    *pairs, here, weight = pl.pallas_call(
        functools.partial(pack_kernel, far),
        out_shape=[like((2, rows, width), queries)] * far
        + [like((rows, width), queries), jax.ShapeDtypeStruct(shape, jnp.bfloat16)],
        in_specs=[SMEM] + [HBM] * 7,
        out_specs=[VMEM] * (far + 2),
        scratch_shapes=[
            pltpu.VMEM((4, *shape), state[0].dtype),
            pltpu.SemaphoreType.DMA((2 * far + 1,)),
            pltpu.SemaphoreType.DMA((4, pieces)),
        ],
        compiler_params=PARAMS,
        cost_estimate=cost(8 * rows * features + 18 * state[0].size),
        name="pack",
    )(me, *map(in_hbm, (keys, values, queries, *state)))
    return pairs, here, weight


def pack_queries_kernel(me_ref, queries, *refs):
    parts, sems = refs[:-1], refs[-1]
    width = parts[0].shape[1]
    copies = [
        pltpu.make_async_copy(
            queries.at[0, :, chip_columns(me_ref, distance, width)], part, sems.at[distance - 1]
        )
        for distance, part in enumerate(parts, 1)
    ]
    for copy in copies:
        copy.start()
    for copy in copies:
        copy.wait()


def pack_queries(me, queries, chips):
    _, rows, features = queries.shape
    width, many = features // chips, chips - 1
    return pl.pallas_call(
        pack_queries_kernel,
        out_shape=[like((rows, width), queries)] * many,
        in_specs=[SMEM, HBM],
        out_specs=[VMEM] * many,
        scratch_shapes=[pltpu.SemaphoreType.DMA((many,))],
        compiler_params=PARAMS,
        cost_estimate=cost(4 * rows * features),
        name="pack_queries",
    )(me, in_hbm(queries))


def merge_kernel(index_ref, *refs):
    pieces, whole = refs[:-1], refs[-1]
    for distance, piece in enumerate(pieces):
        whole[index_ref[0] ^ distance] = piece[...]


def merge(index, pieces):
    return pl.pallas_call(
        merge_kernel,
        out_shape=like((len(pieces), *pieces[0].shape), pieces[0]),
        in_specs=[SMEM] + [VMEM] * len(pieces),
        out_specs=VMEM,
        compiler_params=PARAMS,
        cost_estimate=cost(4 * len(pieces) * pieces[0].size),
        name="merge",
    )(index, *pieces)


def hold_kernel(source, target):
    target[...] = source[...]


def hold(array):
    return pl.pallas_call(
        hold_kernel,
        out_shape=like(array.shape, array),
        in_specs=[VMEM],
        out_specs=VMEM,
        compiler_params=PARAMS,
        cost_estimate=cost(4 * array.size, 3 * 10**10),
        name="hold",
    )(array)


def places(chips, rows, pieces, width):
    tokens = [slice(index * rows, (index + 1) * rows) for index in range(2 * chips)]
    down, out_features = pieces.shape
    first, across = 2 * chips * rows, out_features // width
    weights = [
        slice(first + index * down, first + (index + 1) * down) for index in range(3 * across)
    ]
    return tokens, [weights[index * across : (index + 1) * across] for index in range(3)]


def stack_kernel(chips, *refs):
    pairs, pieces, stacked = refs[:chips], refs[chips:-1], refs[-1]
    rows, width = pairs[0].shape[1:]
    tokens, weights = places(chips, rows, pieces[0], width)
    for distance, pair in enumerate(pairs):
        stacked[tokens[2 * distance], :] = pair[0]
        stacked[tokens[2 * distance + 1], :] = pair[1]
    for piece, blocks in zip(pieces, weights):
        for index, block in enumerate(blocks):
            stacked[block, :] = piece[:, index * width : (index + 1) * width]


def stack(pairs, pieces):
    chips = len(pairs)
    _, rows, width = pairs[0].shape
    total = 2 * chips * rows + len(pieces) * pieces[0].size // width
    return pl.pallas_call(
        functools.partial(stack_kernel, chips),
        out_shape=like((total, width), pairs[0]),
        in_specs=[VMEM] * (chips + len(pieces)),
        out_specs=VMEM,
        compiler_params=PARAMS,
        cost_estimate=cost(4 * total * width),
        name="stack",
    )(*pairs, *pieces)


def collect_kernel(chips, rows, index_ref, own, last, other, weights):
    down, out_features = last.shape
    width = own.shape[1]
    _, blocks = places(chips, rows, last, width)
    for which, stacked in enumerate((own, other)):
        for distance in range(3):
            at = pl.ds(pl.multiple_of((index_ref[0] ^ distance) * down, down), down)
            for index, block in enumerate(blocks[distance]):
                weights[which, at, index * width : (index + 1) * width] = stacked[block, :]
    at = pl.ds(pl.multiple_of((index_ref[0] ^ 3) * down, down), down)
    weights[0, at, :] = last[...]
    weights[1, at, :] = jnp.zeros_like(last)


def collect(index, chips, rows, own, last, other):
    down, out_features = last.shape
    shape = (2, 4 * down, out_features)
    return pl.pallas_call(
        functools.partial(collect_kernel, chips, rows),
        out_shape=like(shape, own),
        in_specs=[SMEM] + [VMEM] * 3,
        out_specs=VMEM,
        compiler_params=PARAMS,
        cost_estimate=cost(0),
        name="collect",
    )(index, own, last, other)


def attend_kernel(distances, chips, me_ref, *refs):
    many = len(distances)
    parts, (own, other, attended, queries, result) = refs[:many], refs[many:]
    total, width = queries.shape
    rows = total // many
    half = width // 2
    chip, core = me_ref[0] // 2, me_ref[0] % 2
    scale = HEAD_DIM ** (-0.5) * math.log2(math.e)

    def attend_from(here):
        order = sorted(here ^ distance for distance in distances)
        place = {chip: index * rows for index, chip in enumerate(order)}
        for distance, part in zip(distances, parts):
            at = place[here ^ distance]
            queries[at : at + rows, :] = part[...]
        row = lax.broadcasted_iota(jnp.int32, (rows, 2 * rows), 0)
        column = lax.broadcasted_iota(jnp.int32, (rows, 2 * rows), 1)
        causal = jnp.where(column < rows, row, 2 * rows * core - 1) >= column

        def both(index, columns):
            at = slice(index * rows, (index + 1) * rows)
            return jnp.concatenate([own[at, columns], other[at, columns]], axis=0)

        ones = jnp.ones((2 * rows, LANES), own.dtype)
        def score_tiles(columns):
            tiles = []
            for c in range(order[-1] + 1):
                first = min(place[chip] for chip in order if chip >= c)
                score = lax.dot_general(
                    queries[first : many * rows, columns],
                    both(2 * (here ^ c), columns),
                    (((1,), (1,)), ((), ())),
                    preferred_element_type=jnp.float32,
                )
                if c in place:
                    masked = jnp.where(causal, score[:rows], -jnp.inf)
                    later = [score[rows:]] if first + rows < many * rows else []
                    score = jnp.concatenate([masked, *later], axis=0)
                tiles.append((c, first, score))
            return tiles

        def exponentials(tiles):
            highest = []
            for chip in order:
                best = None
                for c, first, score in tiles:
                    if c <= chip:
                        at = place[chip] - first
                        block = score[at : at + rows]
                        best = block if best is None else jnp.maximum(best, block)
                highest.append(jnp.max(best, axis=1, keepdims=True))
            highest = jnp.concatenate(highest, axis=0)
            return [
                (c, first, jnp.exp2((score - highest[first:]) * scale).astype(jnp.bfloat16))
                for c, first, score in tiles
            ]

        def combine(columns, tiles):
            totals, start = None, 0
            for c, first, expons in tiles:
                seen = jnp.concatenate([both(2 * (here ^ c) + 1, columns), ones], axis=1)
                total = jnp.dot(expons, seen, preferred_element_type=jnp.float32)
                totals = total if totals is None else totals[first - start :] + total
                start = first
                if c in place:
                    result[first : first + rows, columns] = (
                        totals[:rows, :HEAD_DIM] / totals[:rows, HEAD_DIM:]
                    ).astype(result.dtype)

        heads = [
            slice(head * HEAD_DIM, (head + 1) * HEAD_DIM) for head in range(width // HEAD_DIM)
        ]
        scores = [score_tiles(columns) for columns in heads]
        for columns, tiles in zip(heads, scores):
            combine(columns, exponentials(tiles))
        for index, distance in enumerate(distances):
            at = place[here ^ distance]
            for part in range(2):
                attended[part, index * rows : (index + 1) * rows, :] = result[
                    at : at + rows, part * half : (part + 1) * half
                ]

    for here in range(chips):
        pl.when(chip == here)(functools.partial(attend_from, here))


def attend(me, distances, parts, own, other, chips):
    rows, width = parts[0].shape[-2:]
    length = 2 * chips * rows
    total = len(parts) * rows
    return pl.pallas_call(
        functools.partial(attend_kernel, distances, chips),
        out_shape=like((2, total, width // 2), own),
        in_specs=[SMEM] + [VMEM] * (len(parts) + 2),
        out_specs=VMEM,
        scratch_shapes=[pltpu.VMEM((total, width), own.dtype)] * 2,
        compiler_params=PARAMS,
        cost_estimate=cost(0, 10**10 * (len(distances) - 1)),
        name="attend",
    )(me, *parts, own, other)


def project_kernel(chips, held, me_ref, index_ref, attended, weights, last, *refs):
    outs, other = refs[held:-1], refs[-1]
    down = last.shape[0]
    core = me_ref[0] % 2
    other[...] = weights[1]
    other[pl.ds(pl.multiple_of((index_ref[0] ^ 3) * down, down), down), :] = last[...]
    product = jnp.dot(attended[core], weights[0], preferred_element_type=jnp.float32)
    product += jnp.dot(attended[1 - core], other[...], preferred_element_type=jnp.float32)
    rows = outs[0].shape[0]

    def give(out, distance):
        out[...] = product[distance * rows : (distance + 1) * rows].astype(out.dtype)

    if len(outs) == 1:
        give(outs[0], 0)
        return
    for out, distance in zip(outs[2:], (0, *straight(chips))):
        give(out, distance)
    for which in range(2):

        @pl.when(core == which)
        def _(which=which):
            give(outs[0], early(chips, which))
            give(outs[1], late(chips, which))


def via(core):
    return 1 + core


def late(chips, core):
    return chips - 1 ^ via(core)


def early(chips, core):
    return late(chips, 1 - core)


def straight(chips):
    return [d for d in range(1, chips - 1) if d not in (late(chips, 0), late(chips, 1))]


def project(me, index, attended, weights, last, chips, kinds, held=()):
    _, total, features = attended.shape
    width = weights.shape[2]
    return pl.pallas_call(
        functools.partial(project_kernel, chips, len(held)),
        out_shape=[jax.ShapeDtypeStruct((total // len(kinds), width), kind) for kind in kinds],
        in_specs=[SMEM] * 2 + [VMEM] * (3 + len(held)),
        out_specs=[VMEM] * len(kinds),
        scratch_shapes=[pltpu.VMEM(weights.shape[1:], weights.dtype)],
        compiler_params=PARAMS,
        cost_estimate=cost(0),
        name="project",
    )(me, index, attended, weights, last, *held)


def add_kernel(product, passed, out):
    out[...] = (product[...] + passed[...].astype(jnp.float32)).astype(out.dtype)


def add(product, passed):
    return pl.pallas_call(
        add_kernel,
        out_shape=like(passed.shape, passed),
        in_specs=[VMEM] * 2,
        out_specs=VMEM,
        compiler_params=PARAMS,
        cost_estimate=cost(8 * product.size),
        name="add",
    )(product, passed)


def make_body(seq_count, dp_count):
    chips = seq_count // 2
    far = chips - 1

    def by_core(part, distance):
        return lax.ppermute(
            part, "seq", [(i, i ^ 2 * distance(i % 2)) for i in range(seq_count)]
        )

    def to_chip(part, distance):
        return swap(part, "seq", seq_count, 2 * distance)

    def exchange(parts):
        got = [to_chip(part, d) if d else part for d, part in enumerate(parts)]
        return [*got[:-1], lax.optimization_barrier(got[-1])]

    def body(queries, keys, values, master, moment, second, gradient):
        rows = queries.shape[1]
        out_features = master.shape[1]
        me = lax.axis_index("seq").astype(jnp.int32).reshape(1)
        place = lax.axis_index("dp").astype(jnp.int32)

        farthest = pack_far(me, keys, values, chips)
        near_keys, farthest = lax.optimization_barrier((keys, farthest))
        state = (master, moment, second, gradient)
        sent_pairs, own_queries, weight = pack(me, near_keys, values, queries, state, chips)
        sent_pairs.append(farthest)
        pairs = exchange(sent_pairs)

        weight = weight[None]
        span = 1
        while 4 * span < dp_count:
            many = 4 if dp_count // span % 16 == 0 else 2
            pieces = [weight] + [swap(weight, "dp", dp_count, span * d) for d in range(1, many)]
            weight = merge((place // span % many).reshape(1), pieces)
            weight = weight.reshape(-1, *weight.shape[2:])
            span *= many
        weight = weight.reshape(-1, out_features)
        pieces = [weight] + [swap(weight, "dp", dp_count, span * d) for d in (1, 2)]
        queries, _ = lax.optimization_barrier((queries, weight))
        sent_queries = pack_queries(me, queries, chips)
        pieces[2], sent_queries = lax.optimization_barrier((pieces[2], sent_queries))
        own = stack(pairs, pieces)
        forwarded = hold(swap(pieces[2], "dp", dp_count, span))

        other = swap(own, "seq", seq_count, 1)
        sent_queries, _ = lax.optimization_barrier((sent_queries, own))
        near_parts, forwarded = lax.optimization_barrier((sent_queries[:-1], forwarded))
        sent_queries = [*near_parts, sent_queries[-1]]
        own_queries = exchange([own_queries, *sent_queries])

        attended = attend(me, (far,), own_queries[far:], own, other, chips)
        near_queries, others = own_queries[:far], swap(forwarded, "seq", seq_count, 1)
        index = (place // span % 4).reshape(1)
        weights = collect(index, chips, rows, own, forwarded, other)
        (product,) = project(
            me, index, attended, weights, others, chips, [attended.dtype], own_queries[far:]
        )
        passed = by_core(product, via)
        attended = attend(me, tuple(range(far)), near_queries, own, other, chips)
        kinds = [attended.dtype, jnp.float32, jnp.float32] + [attended.dtype] * (chips - 4)
        sent, waiting, projected, *rest = project(
            me, index, attended, weights, others, chips, kinds, near_queries
        )
        got = [by_core(sent, functools.partial(early, chips))]
        got += [to_chip(product, d) for d, product in zip(straight(chips), rest)]
        for product in got:
            projected += product.astype(jnp.float32)
        projected = lax.optimization_barrier(projected)
        last = by_core(add(waiting, passed), functools.partial(late, chips))
        projected += last.astype(jnp.float32)
        projected = projected.astype(jnp.bfloat16)[None]
        return (projected, adamw(master, moment, second, gradient))

    return body


def solution(mesh):
    tokens = P("dp", "seq", None)
    rows = P(("seq", "dp"), None)
    return jax.shard_map(
        make_body(mesh.shape["seq"], mesh.shape["dp"]),
        mesh=mesh,
        in_specs=(tokens,) * 3 + (rows,) * 4,
        out_specs=(tokens, rows),
        check_vma=False,
    )
```
